512 devices in a mesh: ctx: 64 (over x, y, core), ch: 8 (over z).
Axes of the slice: x: 4, y: 8, z: 8, core: 2. Of those that a mesh axis runs over, the one named last changes fastest.
Arguments:
- features: bfloat16 [10240, 3, 4096], P('ctx', None, 'ch'), may hold values from -6 to 6
- segment_ids: int32 [10240], P('ctx'), may hold values from 0 to 63, never falling along the last dimension, each value on 1 to 320 neighbouring positions
- feat_taps: float32 [3, 3, 4096], P(None, None, 'ch'), may hold values from -3 to 3
- mixer_filter: float32 [256, 128], P('ch'), may hold values from -0.5 to 0.5
- skip_gain: float32 [4096], P('ch'), may hold values from 0.5 to 1.5
- out_weight: bfloat16 [4096, 8192], P('ctx', 'ch'), may hold values from -0.09375 to 0.09375
- targets: int32 [10240], P('ctx'), may hold values from 0 to 63, as said below
- row_costs: int32 [10240], P('ctx'), may hold values from 1 to 160
Outputs:
- relaid_out: bfloat16 [10240, 8192], P('ctx', 'ch')
- shard_cost: float32 [64], P('ctx')
The draws below stay inside these ranges and needn't reach their ends.
Inputs may be any that keep to these rules, and one draw needn't show every extreme that they name: `segment_ids`: never fall along the rows. `targets`: each shard sends exactly 5 of its rows to each of 32 target shards and none to the others; every shard receives exactly 160 rows.
All inputs are finite; a program needn't handle non-finite values.
Results may differ from the reference program's by a relative error of at most 0.014.
Values may be sent and summed in bfloat16 or wider, within the bound.
A program may use at most 64 MiB of HBM per device.

```python
import math
import jax
import jax.numpy as jnp
import numpy as np
from jax import lax

C = 4096
DOUT = 8192
GROUP = 16
TAPS = 128
TOK_DEV = 160
GROUPS = 256
TOKENS = 10240
SHARDS = 64
CAP = 5


def draw_targets(key, part):
    key = jax.random.fold_in(key, 5)
    shift_key, order_key = jax.random.split(key)
    group_count = TOK_DEV // CAP
    values = jnp.arange(SHARDS, dtype=jnp.int32)
    scores = jax.random.permutation(shift_key, SHARDS).astype(jnp.int32)
    scores = jnp.where(values == 1, -2, jnp.where(values == SHARDS // 2, -1, scores))
    shifts = jnp.argsort(scores, stable=True)[:group_count].astype(jnp.int32)
    order_keys = jax.random.split(order_key, SHARDS)
    orders = jax.vmap(lambda one_key: jax.random.permutation(one_key, TOK_DEV))(order_keys)
    group_of = orders // CAP
    source = jnp.arange(SHARDS, dtype=jnp.int32)[:, None]
    return ((source + shifts[group_of]) % SHARDS).reshape(-1).astype(jnp.int32)


def draw_row_costs(key, part):
    key = jax.random.fold_in(key, 9)
    value_key, spot_key = jax.random.split(key)
    position = jnp.arange(TOKENS, dtype=jnp.int32)
    ceiling = 33 + 128 * position // TOKENS
    draw_values = jax.random.randint(value_key, (TOKENS,), 1, ceiling)
    chosen = TOKENS - 1 - jax.random.randint(spot_key, (), 0, TOK_DEV)
    return jnp.where(position == chosen, 160, draw_values).astype(jnp.int32)


def shard_levels(rng, dims, shards, least, top_value):
    gain = 1.0
    for dim, shards_of in shards:
        draws = jax.random.uniform(jax.random.fold_in(jax.random.fold_in(rng, 6), dim), (shards_of,), jnp.float32, least / len(shards), top_value / len(shards))
        gain = gain * jnp.repeat(jnp.exp(draws), dims[dim] // shards_of).reshape((-1,) + (1,) * (len(dims) - 1 - dim))
    return gain


def length_profile(count, total, bound, slope):
    loads = [(1 << 20) // math.isqrt(grade ** slope) + 1 for grade in range(2, count + 1)]
    rest, given = total - bound - (count - 1), [1] * (count - 1)
    while rest > 0:
        free = [i for i in range(count - 1) if given[i] < bound]
        pool, remaining = sum([loads[i] for i in free]), rest
        for i in free:
            extra = min(bound - given[i], max(1, remaining * loads[i] // pool), rest)
            given[i] = given[i] + extra
            rest = rest - extra
    return np.array([bound] + given)


def uneven(rng, amount, total, limit, skew):
    if amount == 2:
        one = jax.random.randint(rng, (), max(1, total - limit), min(limit, total - 1) + 1)
        return jnp.stack([one, total - one])
    tallies = jnp.asarray(length_profile(amount, total, limit, skew), jnp.int32)
    couples = (amount - 1) // 2
    giver, taker = tallies[1:1 + 2 * couples:2], tallies[2:2 + 2 * couples:2]
    slack = jnp.minimum(giver - 1, limit - taker)
    moved = jax.random.randint(jax.random.fold_in(rng, 1), (couples,), 0, 1 << 20) % (slack + 1)
    tallies = tallies.at[1:1 + 2 * couples:2].set(giver - moved).at[2:2 + 2 * couples:2].set(taker + moved)
    return tallies[jax.random.permutation(jax.random.fold_in(rng, 2), amount)]


def normal_values(stream_key, extent, width, most, cuts=(), kind=jnp.bfloat16):
    level = shard_levels(stream_key, extent, cuts, -0.22, 0.18) if cuts else 1.0
    values = jax.random.normal(stream_key, extent, jnp.float32) * width * level
    return jnp.minimum(jnp.maximum(values, -most), most).astype(kind)


def setup_inputs(seed: int = 0) -> dict:
    arg_keys = jax.random.split(jax.random.key(seed), 9)
    return {
        "features": normal_values(arg_keys[0], (TOKENS, 3, C), 1.0, 6.0, ((0, 64), (2, 8))),
        "segment_ids": jnp.searchsorted(jnp.cumsum(uneven(arg_keys[1], SHARDS, TOKENS, 2 * TOK_DEV, 2)), jnp.arange(TOKENS), side="right").astype(jnp.int32),
        "feat_taps": normal_values(arg_keys[2], (3, 3, C), 0.6, 3.0, ((2, 8),), jnp.float32),
        "mixer_filter": normal_values(arg_keys[3], (GROUPS, TAPS), TAPS ** -0.5, 0.5, ((0, 8),), jnp.float32),
        "skip_gain": jnp.clip(0.5 + 1.0 * jax.random.uniform(arg_keys[4], (C,), jnp.float32) ** shard_levels(arg_keys[4], (C,), ((0, 8),), -0.2, 0.2), 0.5, 1.5),
        "out_weight": normal_values(arg_keys[5], (C, DOUT), C ** -0.5, 0.09375, ((0, 64), (1, 8))),
        "targets": draw_targets(jax.random.fold_in(arg_keys[8], 71), 0),
        "row_costs": draw_row_costs(jax.random.fold_in(arg_keys[8], 71), 0),
    }


def delayed(signal, steps):
    padding = jnp.zeros((steps,) + signal.shape[1:], signal.dtype)
    return jnp.concatenate([padding, signal[:-steps]], axis=0)


def same_as(segment_ids, steps):
    earlier = jnp.concatenate([jnp.full((steps,), -1, jnp.int32), segment_ids[:-steps]])
    return (earlier == segment_ids).astype(jnp.float32)[:, None]


def reference(features, segment_ids, feat_taps, mixer_filter, skip_gain, out_weight, targets, row_costs):
    match_one = same_as(segment_ids, 1)
    match_two = same_as(segment_ids, 2)

    def featurize(index):
        signal = features[:, index, :].astype(jnp.float32)
        tap_weights = feat_taps[index]
        return (tap_weights[0][None, :] * signal
                + tap_weights[1][None, :] * delayed(signal, 1) * match_one
                + tap_weights[2][None, :] * delayed(signal, 2) * match_two)

    feat_q = featurize(0)
    feat_k = featurize(1)
    feat_v = featurize(2)
    mixer_in = (feat_k * feat_v).astype(jnp.bfloat16)
    rounded = lax.optimization_barrier(mixer_filter.astype(jnp.bfloat16)).astype(jnp.float32)
    per_channel = jnp.repeat(rounded, GROUP, axis=0).T
    signal = mixer_in.astype(jnp.float32)
    padded = jnp.concatenate([jnp.zeros((TAPS - 1, C), jnp.float32), signal], axis=0)
    padded_seg = jnp.concatenate([jnp.full((TAPS - 1,), -1, jnp.int32), segment_ids])

    def tap_step(running, tap_index):
        offset_row = (TAPS - 1 - tap_index).astype(jnp.int32)
        moved_rows = lax.dynamic_slice_in_dim(padded, offset_row, TOKENS, 0)
        moved_seg = lax.dynamic_slice_in_dim(padded_seg, offset_row, TOKENS, 0)
        weight_row = lax.dynamic_index_in_dim(per_channel, tap_index, 0, keepdims=False)
        keep_mask = (moved_seg == segment_ids).astype(jnp.float32)[:, None]
        return running + weight_row[None, :] * moved_rows * keep_mask, None

    filtered, unused = lax.scan(tap_step, jnp.zeros((TOKENS, C), jnp.float32), jnp.arange(TAPS, dtype=jnp.int32))
    gated_rows = (feat_q * (filtered + skip_gain[None, :] * signal)).astype(jnp.bfloat16)
    projected = jnp.dot(gated_rows, out_weight, preferred_element_type=jnp.float32).astype(jnp.bfloat16)
    row_order = jnp.argsort(targets, stable=True)
    relaid_out = projected[row_order]
    summed = jax.ops.segment_sum(row_costs, targets, num_segments=SHARDS)
    shard_cost = summed.astype(jnp.float32) / (32.0 * TOK_DEV)
    return relaid_out, shard_cost
```

```python
import functools

import jax
import jax.numpy as jnp
from jax import lax
from jax.experimental import pallas as pl
from jax.experimental.pallas import tpu as pltpu
from jax.sharding import PartitionSpec as P

MESH = pl.DeviceIdType.MESH
BF = jnp.bfloat16
F32 = jnp.float32
ROWS = 160
TAPS = 128
UNITS = 2
ACOLS = 128
BCOLS = 384


def place():
    ctx = lax.axis_index("ctx")
    return ctx // 16, (ctx // 2) % 8, ctx % 2, lax.axis_index("ch"), ctx


def offset_of(j):
    return ((j + 1) // 2) * (2 * (j % 2) - 1)


def iota(shape, dim):
    return lax.broadcasted_iota(jnp.int32, shape, dim)


def mixer_kernel(
    feat_in, w_in, taps, filt, gain, meta, metac,
    out, cost_out,
    feat, qf, win, hrev, mask_s, gsend, gbuf, cbuf, slots, prevmeta,
    packed, arrived, dmat, abuf, wa, wb, acc, osend, orecv,
    s_feat, s_loc, s_sib, r_sib, s_halo, r_halo, s_gx, r_gx, s_rel, r_rel, s_self,
    s_ax, r_ax, s_ay, r_ay, s_by, r_by, s_bx, r_bx, s_bx2, r_bx2,
    s_z, r_z, s_c, r_c, s_o, r_o,
):
    x, y, k, z, ctx = place()
    chip = x * 8 + y
    kk = 1 - k

    def dev(dx=0, dy=0, dz=0, dk=0):
        return (
            (((x + dx + 4) % 4) * 8 + (y + dy + 8) % 8) * 2 + (k + dk) % 2,
            (z + dz + 8) % 8,
        )

    sibling = dev(dk=1)
    following = ((ctx + 1) % 64, z)
    previous = ((ctx + 63) % 64, z)
    pending = []

    def send(src, dst, ssem, rsem, to):
        c = pltpu.make_async_remote_copy(
            src_ref=src, dst_ref=dst, send_sem=ssem, recv_sem=rsem,
            device_id=to, device_id_type=MESH,
        )
        c.start()
        pending.append(c)

    def arrived_at(dst, ssem, rsem):
        pltpu.make_async_remote_copy(
            src_ref=dst, dst_ref=dst, send_sem=ssem, recv_sem=rsem,
            device_id=sibling, device_id_type=MESH,
        ).wait_recv()

    load = pltpu.make_async_copy(feat_in, feat.at[:, pl.ds(16, ROWS)], s_feat)
    load.start()
    barrier = pltpu.get_barrier_semaphore()

    def greet(i, carry):
        other = (chip + i) % 32
        pl.semaphore_signal(barrier, inc=1, device_id=(other * 2 + k, z), device_id_type=MESH)
        return carry

    lax.fori_loop(1, 32, greet, 0)
    for to in (sibling, following, previous, dev(dz=1), dev(dz=-1)):
        pl.semaphore_signal(barrier, inc=1, device_id=to, device_id_type=MESH)

    own_a = wa.at[y, x]
    own_b = wb.at[x, y]
    mine = pl.ds(pl.multiple_of(k * 64, 64), 64)

    def wcols(core, first, count):
        return w_in.at[:, pl.ds(pl.multiple_of(core * 512 + first, 128), count)]

    loc_a = pltpu.make_async_copy(wcols(k, 0, ACOLS), own_a.at[mine], s_loc.at[0])
    loc_b = pltpu.make_async_copy(wcols(k, ACOLS, BCOLS), own_b.at[mine], s_loc.at[1])
    loc_a.start()
    loc_b.start()

    seg_col = metac[:, 0:1]
    tgt_col = metac[:, 1:2]
    cost_col = metac[:, 2:3]
    lag = iota((ROWS, 384), 0) + TAPS - iota((ROWS, 384), 1)
    in_reach = (lag >= 0) & (lag < TAPS)

    def same_segment(prev_row):
        seg_row = jnp.concatenate([prev_row, meta[0:1, :]], axis=1)
        return jnp.where(in_reach & (seg_col == seg_row), 1.0, 0.0)

    def featurize(index, center, match_one, match_two):
        return (
            taps[index, 0:1, :] * center
            + taps[index, 1:2, :] * pltpu.roll(center, 1, 0) * match_one
            + taps[index, 2:3, :] * pltpu.roll(center, 2, 0) * match_two
        )

    seg_own = same_segment(jnp.full((1, 128), -1.0, F32))
    back = jnp.sum(seg_own, axis=1, keepdims=True)
    m_one = jnp.where(back > 1.5, 1.0, 0.0)
    m_two = jnp.where(back > 2.5, 1.0, 0.0)
    load.wait()
    own_rows = pl.ds(16, ROWS)
    qf[...] = featurize(0, feat[0, own_rows].astype(F32), m_one, m_two)
    win[pl.ds(128, ROWS), :] = (
        featurize(1, feat[1, own_rows].astype(F32), m_one, m_two)
        * featurize(2, feat[2, own_rows].astype(F32), m_one, m_two)
    ).astype(BF)
    win[pl.ds(288, 96), :] = jnp.zeros((96, 512), BF)

    tgt_row = meta[1:2, :]
    same_target = tgt_col == tgt_row
    rq = iota((ROWS, 256), 0)
    rr = iota((ROWS, 256), 1)
    rank_row = jnp.sum(jnp.where(same_target & (rq < rr), 1.0, 0.0), axis=0, keepdims=True)
    rank_col = jnp.sum(jnp.where(same_target & (rr < rq), 1.0, 0.0), axis=1, keepdims=True)
    kf = k.astype(F32)
    chip_row = jnp.floor(tgt_row * 0.5)
    chip_col = jnp.floor(tgt_col * 0.5)
    lane_row = (tgt_row - 2.0 * chip_row) * 10.0 + kf * 5.0 + rank_row
    lane_col = (tgt_col - 2.0 * chip_col) * 10.0 + kf * 5.0 + rank_col
    slots[k, 0:1, :] = chip_row * 32.0 + lane_row
    slots[k, 1:2, :] = chip_row * 32.0 + 20.0
    mine_rows = pl.ds(pl.multiple_of(k * ROWS, 16), ROWS)
    cbuf[mine_rows, :] = jnp.where(
        iota((ROWS, 128), 1).astype(F32) == lane_col, cost_col, 0.0
    ).astype(BF)

    flip = (iota((TAPS, TAPS), 0) + iota((TAPS, TAPS), 1)) % TAPS == 0
    hrev[...] = jnp.dot(
        filt[...].astype(BF), jnp.where(flip, 1.0, 0.0).astype(BF), preferred_element_type=F32
    )

    pl.semaphore_wait(barrier, 36)

    send(wcols(kk, 0, ACOLS), own_a.at[mine], s_sib.at[0], r_sib.at[0], sibling)
    send(wcols(kk, ACOLS, BCOLS), own_b.at[mine], s_sib.at[1], r_sib.at[1], sibling)
    send(feat.at[:, pl.ds(160, 16)], feat.at[:, pl.ds(0, 16)], s_halo.at[0], r_halo.at[0], following)
    send(meta, prevmeta, s_halo.at[1], r_halo.at[1], following)
    send(win.at[pl.ds(160, 128)], win.at[pl.ds(0, 128)], s_halo.at[2], r_halo.at[2], following)
    send(slots.at[k], slots.at[k], s_gx.at[1], r_gx.at[1], sibling)
    send(cbuf.at[mine_rows], cbuf.at[mine_rows], s_gx.at[2], r_gx.at[2], sibling)

    events = []

    def at(when, what, *args):
        events.append((when, len(events), functools.partial(what, *args)))

    def w_own():
        theirs = pl.ds(pl.multiple_of(kk * 64, 64), 64)
        loc_a.wait()
        loc_b.wait()
        arrived_at(own_a.at[theirs], s_sib.at[0], r_sib.at[0])
        arrived_at(own_b.at[theirs], s_sib.at[1], r_sib.at[1])
        for d in (1, 2, 3):
            send(own_a, own_a, s_ax.at[d - 1], r_ax.at[d - 1], dev(dx=d))
        by_send(1)
        bx_send(0)

    def by_piece(t, way):
        ref = wb.at[x, (y + (1 - t if way == 0 else t - 1) + 8) % 8]
        return ref if t < 4 else ref.at[pl.ds(way * 64, 64)]

    def by_landed(t, way):
        ref = wb.at[x, (y + (-t if way == 0 else t) + 8) % 8]
        return ref if t < 4 else ref.at[pl.ds(way * 64, 64)]

    def by_send(t):
        for way in (0, 1):
            piece = by_piece(t, way)
            send(piece, piece, s_by.at[way, t - 1], r_by.at[way, t - 1], dev(dy=1 - 2 * way))

    def by_step(t):
        for way in (0, 1):
            arrived_at(by_landed(t, way), s_by.at[way, t - 1], r_by.at[way, t - 1])
        if t < 4:
            by_send(t + 1)
            bx_send(2 * t - 1)
            bx_send(2 * t)
        else:
            bx_send(7)

    def ay_piece(t, way):
        ref = wa.at[(y + (1 - t if way == 0 else t - 1) + 8) % 8]
        return ref if t < 4 else ref.at[pl.ds(way * 2, 2)]

    def ay_landed(t, way):
        ref = wa.at[(y + (-t if way == 0 else t) + 8) % 8]
        return ref if t < 4 else ref.at[pl.ds(way * 2, 2)]

    def ay_send(t):
        for way in (0, 1):
            piece = ay_piece(t, way)
            send(piece, piece, s_ay.at[way, t - 1], r_ay.at[way, t - 1], dev(dy=1 - 2 * way))

    def ax_done():
        for d in (1, 2, 3):
            arrived_at(wa.at[y, (x - d + 4) % 4], s_ax.at[d - 1], r_ax.at[d - 1])
        ay_send(1)

    def ay_step(t):
        for way in (0, 1):
            arrived_at(ay_landed(t, way), s_ay.at[way, t - 1], r_ay.at[way, t - 1])
        if t < 4:
            ay_send(t + 1)

    def bx_row(j):
        return (y + offset_of(j) + 8) % 8

    def bx_send(j):
        piece = wb.at[x, bx_row(j)]
        for way in (0, 1):
            send(piece, piece, s_bx.at[way, j], r_bx.at[way, j], dev(dx=1 - 2 * way))

    def bx_step(j):
        for way in (0, 1):
            landed = wb.at[(x + 2 * way - 1 + 4) % 4, bx_row(j)]
            arrived_at(landed, s_bx.at[way, j], r_bx.at[way, j])
        way = j % 2
        piece = wb.at[(x + 2 * way - 1 + 4) % 4, bx_row(j)]
        send(piece, piece, s_bx2.at[j], r_bx2.at[j], dev(dx=1 - 2 * way))

    def bx_last(j):
        arrived_at(wb.at[(x + 2) % 4, bx_row(j)], s_bx2.at[j], r_bx2.at[j])

    def halo():
        arrived_at(prevmeta, s_halo.at[1], r_halo.at[1])
        arrived_at(feat.at[:, pl.ds(0, 16)], s_halo.at[0], r_halo.at[0])
        prev_row = jnp.where(ctx == 0, -1.0, prevmeta[3:4, 0:128])
        mask = same_segment(prev_row)
        mask_s[...] = mask
        count = jnp.sum(mask[0:32], axis=1, keepdims=True)[0:16]
        one = jnp.where(count > 1.5, 1.0, 0.0)
        two = jnp.where(count > 2.5, 1.0, 0.0)
        pad = jnp.zeros((16, 1), F32)
        one = jnp.concatenate([pad, one], axis=0)
        two = jnp.concatenate([pad, two], axis=0)
        fixed = [
            featurize(i, feat[i, pl.ds(0, 32)].astype(F32), one, two)[16:32] for i in range(3)
        ]
        qf[pl.ds(0, 16), :] = fixed[0]
        win[pl.ds(128, 16), :] = (fixed[1] * fixed[2]).astype(BF)
        arrived_at(win.at[pl.ds(0, 128)], s_halo.at[2], r_halo.at[2])

    def conv(part):
        cols = pl.ds(pl.multiple_of(part * 256, 256), 256)
        window = win[:, cols]
        lane_group = iota((ROWS, 256), 1) // 16

        def step(i, total):
            stack = []
            for n in range(4):
                row = jnp.broadcast_to(hrev[pl.ds(part * 16 + i * 4 + n, 1), :], (TAPS, TAPS))
                turned = pltpu.roll(row, 0, 1, stride=1, stride_axis=0)
                tall = jnp.concatenate([turned, turned[0:32]], axis=0)
                wide = jnp.concatenate([tall, tall, tall], axis=1)
                stack.append(jnp.where(mask_s[...] > 0.5, wide, 0.0).astype(BF))
            res = jnp.dot(jnp.concatenate(stack, axis=0), window, preferred_element_type=F32)
            for n in range(4):
                total = jnp.where(
                    lane_group == i * 4 + n, res[n * ROWS:(n + 1) * ROWS], total
                )
            return total

        total = lax.fori_loop(0, 4, step, jnp.zeros((ROWS, 256), F32))
        center = win[pl.ds(128, ROWS), cols].astype(F32)
        return (qf[:, cols] * (total + gain[:, cols] * center)).astype(BF)

    def conv_theirs():
        gsend[...] = conv(kk)
        send(gsend, gbuf.at[mine_rows], s_gx.at[0], r_gx.at[0], sibling)

    def conv_mine():
        gbuf[mine_rows, :] = conv(k)

    def unit_cols(u):
        return pl.ds(u * 128, 128)

    def pack(u):
        if u == 0:
            other_rows = pl.ds(pl.multiple_of(kk * ROWS, 16), ROWS)
            arrived_at(slots.at[kk], s_gx.at[1], r_gx.at[1])
            arrived_at(cbuf.at[other_rows], s_gx.at[2], r_gx.at[2])
            arrived_at(gbuf.at[other_rows], s_gx.at[0], r_gx.at[0])
        slot = jnp.concatenate([slots[0, 0:1, 0:ROWS], slots[1, 0:1, 0:ROWS]], axis=1)
        place_row = iota((1024, 2 * ROWS), 0).astype(F32)
        pick = jnp.where(place_row == slot, 1.0, 0.0).astype(BF)
        res = jnp.dot(pick, gbuf[:, unit_cols(u)], preferred_element_type=F32)
        if u == 0:
            cslot = jnp.concatenate([slots[0, 1:2, 0:ROWS], slots[1, 1:2, 0:ROWS]], axis=1)
            cpick = jnp.where(place_row == cslot, 1.0, 0.0).astype(BF)
            res = res + jnp.dot(cpick, cbuf[...], preferred_element_type=F32)
        packed[u] = res.astype(BF)

        block = pl.ds(pl.multiple_of(chip * 32, 32), 32)
        pltpu.make_async_copy(packed.at[u, block], arrived.at[u, block], s_self.at[u]).start()

        def post(i, carry):
            dx = i % 4
            dy = offset_of(i // 4)
            other = ((x + dx) % 4) * 8 + (y + dy + 8) % 8
            theirs = pl.ds(pl.multiple_of(other * 32, 32), 32)
            pltpu.make_async_remote_copy(
                src_ref=packed.at[u, theirs], dst_ref=arrived.at[u, block],
                send_sem=s_rel.at[u], recv_sem=r_rel.at[u],
                device_id=(other * 2 + k, z), device_id_type=MESH,
            ).start()
            return carry

        lax.fori_loop(1, 32, post, 0)

    def relay_wait(u):
        block = pl.ds(pl.multiple_of(chip * 32, 32), 32)
        bulk = pltpu.make_async_remote_copy(
            src_ref=packed.at[u, pl.ds(0, 992)], dst_ref=arrived.at[u, pl.ds(0, 992)],
            send_sem=s_rel.at[u], recv_sem=r_rel.at[u],
            device_id=sibling, device_id_type=MESH,
        )
        bulk.wait_send()
        bulk.wait_recv()
        pltpu.make_async_copy(packed.at[u, block], arrived.at[u, block], s_self.at[u]).wait()

    def unpack(u):
        relay_wait(u)
        if u == 0:
            pickc = jnp.where(iota((32, 1024), 1) == iota((32, 1024), 0) * 32 + 20, 1.0, 0.0)
            costs = jnp.dot(pickc.astype(BF), arrived[0], preferred_element_type=F32)
            live = jnp.where(costs > 0.5, 1.0, 0.0)
            lane = iota((32, 128), 1)
            own = (lane >= k * 10) & (lane < k * 10 + 10)
            total = jnp.sum(jnp.where(own, costs, 0.0)) / (32.0 * ROWS)
            cost_out[...] = jnp.broadcast_to(total, (8, 128))
            a = iota((128, 128), 0)
            b = iota((128, 128), 1)
            both = (a // 10 == b // 10) & (a % 5 == 0) & (b < 20)
            first = both & (a % 10 == 0) & (b % 10 >= 5)
            live_b = live.astype(BF)
            tally = jnp.dot(live_b, jnp.where(both, 1.0, 0.0).astype(BF), preferred_element_type=F32)
            before = jnp.dot(live_b, jnp.where(first, 1.0, 0.0).astype(BF), preferred_element_type=F32)
            lower = jnp.where(iota((32, 32), 1) < iota((32, 32), 0), 1.0, 0.0)
            rank = jnp.dot(lower.astype(BF), tally.astype(BF), preferred_element_type=F32) + before
            code = jnp.where(live > 0.5, rank + 1.0, 0.0)
            spread = jnp.where(iota((128, 1024), 0) == iota((128, 1024), 1) % 32, 1.0, 0.0)
            wide = jnp.dot(code.astype(BF), spread.astype(BF), preferred_element_type=F32)
            mine_only = iota((32, 1024), 0) == iota((32, 1024), 1) // 32
            code_row = jnp.sum(jnp.where(mine_only, wide, 0.0), axis=0, keepdims=True)
            i_row = iota((1, 1024), 1) % 32
            core_row = i_row // 10
            dest = (core_row * ROWS + i_row % 5).astype(F32) + 5.0 * (code_row - 1.0)
            dest = jnp.where((code_row > 0.5) & (i_row < 20), dest, -1.0)
            hit = iota((2 * ROWS, 1024), 0).astype(F32) == dest
            dmat[...] = jnp.where(hit, 1.0, 0.0).astype(BF)
        rows = jnp.dot(dmat[...], arrived[u], preferred_element_type=F32).astype(BF)
        abuf[z * 2 + k, :, unit_cols(u)] = rows
        z_send(u, 1)
        mine_slot = abuf.at[z * 2 + k, :, unit_cols(u)]
        send(mine_slot, mine_slot, s_c.at[u, 0], r_c.at[u, 0], sibling)

    def z_slot(u, off, core):
        return abuf.at[((z + off + 8) % 8) * 2 + core, :, unit_cols(u)]

    def z_part(ref, t, way):
        return ref if t < 4 else ref.at[pl.ds(way * ROWS, ROWS)]

    def z_send(u, t):
        for way in (0, 1):
            piece = z_part(z_slot(u, 1 - t if way == 0 else t - 1, k), t, way)
            send(piece, piece, s_z.at[u, way, t - 1], r_z.at[u, way, t - 1], dev(dz=1 - 2 * way))

    def z_step(u, t):
        for way in (0, 1):
            landed = z_part(z_slot(u, -t if way == 0 else t, k), t, way)
            arrived_at(landed, s_z.at[u, way, t - 1], r_z.at[u, way, t - 1])
        if t < 4:
            z_send(u, t + 1)
        for j in ((2 * t - 1, 2 * t) if t < 4 else (7,)):
            piece = z_slot(u, offset_of(j), k)
            send(piece, piece, s_c.at[u, j], r_c.at[u, j], sibling)

    def multiply(first, last):
        def step(j, carry):
            zo = (z + offset_of(j) + 8) % 8
            for u in range(UNITS):
                arrived_at(abuf.at[zo * 2 + kk, :, unit_cols(u)], s_c.at[u, j], r_c.at[u, j])
            xs = zo // 2
            for half in (0, 1):
                ys = (zo % 2) * 4 + 2 * half
                part_a = jnp.concatenate([wa[ys, xs], wa[ys + 1, xs]], axis=0)
                part_b = jnp.concatenate([wb[xs, ys], wb[xs, ys + 1]], axis=0)
                weights = jnp.concatenate([part_a, part_b], axis=1)
                acc[...] += jnp.dot(
                    abuf[zo * 2 + half], weights, preferred_element_type=F32
                )
            return carry

        lax.fori_loop(first, last, step, 0)

    def clear():
        acc[...] = jnp.zeros_like(acc)

    def finish():
        theirs = pl.ds(pl.multiple_of(kk * ROWS, 16), ROWS)
        osend[...] = acc[theirs, :].astype(BF)
        send(osend, orecv, s_o, r_o, sibling)
        out[:, pl.ds(pl.multiple_of(k * 512, 512), 512)] = acc[mine_rows, :].astype(BF)
        arrived_at(orecv, s_o, r_o)
        out[:, pl.ds(pl.multiple_of(kk * 512, 512), 512)] = orecv[...]

    at(1.5, w_own)
    at(2.5, halo)
    at(2.6, conv_theirs)
    at(4.0, ax_done)
    at(5.1, conv_mine)
    for t, when in ((1, 5.0), (2, 8.6), (3, 11.0), (4, 13.0)):
        at(when, by_step, t)
    for t, when in ((1, 8.7), (2, 12.0), (3, 16.0), (4, 18.0)):
        at(when, ay_step, t)
    for j in range(8):
        at(5.0 + 2.9 * j, bx_step, j)
        at(8.5 + 2.9 * j, bx_last, j)
    at(8.0, pack, 0)
    at(8.5, pack, 1)
    at(9.0, clear)
    at(15.0, unpack, 0)
    at(20.0, unpack, 1)
    for t in (1, 2, 3, 4):
        at(15.0 + 2.8 * t, z_step, 0, t)
        at(21.0 + 2.8 * t, z_step, 1, t)
    at(31.0, multiply, 0, 7)
    at(33.0, multiply, 7, 8)
    at(40.0, finish)
    for _, _, run in sorted(events, key=lambda e: e[:2]):
        run()
    for c in pending:
        c.wait_send()


def local(features, segment_ids, feat_taps, mixer_filter, skip_gain, out_weight, targets, row_costs):
    parts = jnp.transpose(features, (1, 0, 2))
    seg = segment_ids.astype(F32)
    tgt = targets.astype(F32)
    cost = row_costs.astype(F32)
    pad = (0, 96)
    meta = jnp.stack(
        [
            jnp.pad(seg, pad, constant_values=-7.0),
            jnp.pad(tgt, pad, constant_values=-7.0),
            jnp.pad(cost, pad),
            jnp.pad(seg[32:], (0, 128)),
        ]
        + [jnp.zeros((256,), F32)] * 4
    )
    metac = jnp.stack([seg, tgt, cost], axis=1)
    vmem = pl.BlockSpec(memory_space=pltpu.VMEM)
    hbm = pl.BlockSpec(memory_space=pl.ANY)
    dma = pltpu.SemaphoreType.DMA
    u = UNITS
    flops = 2 * 320 * 4096 * 512
    out, cost_out = pl.pallas_call(
        mixer_kernel,
        out_shape=(
            jax.ShapeDtypeStruct((ROWS, 1024), BF),
            jax.ShapeDtypeStruct((8, 128), F32),
        ),
        in_specs=[hbm, hbm] + [vmem] * 5,
        out_specs=(vmem, vmem),
        scratch_shapes=[
            pltpu.VMEM((3, 16 + ROWS, 512), BF),
            pltpu.VMEM((ROWS, 512), F32),
            pltpu.VMEM((384, 512), BF),
            pltpu.VMEM((32, 128), F32),
            pltpu.VMEM((ROWS, 384), F32),
            pltpu.VMEM((ROWS, 256), BF),
            pltpu.VMEM((2 * ROWS, 256), BF),
            pltpu.VMEM((2 * ROWS, 128), BF),
            pltpu.VMEM((2, 8, 256), F32),
            pltpu.VMEM((8, 256), F32),
            pltpu.VMEM((u, 1024, 128), BF),
            pltpu.VMEM((u, 1024, 128), BF),
            pltpu.VMEM((2 * ROWS, 1024), BF),
            pltpu.VMEM((16, 2 * ROWS, 256), BF),
            pltpu.VMEM((8, 4, 128, ACOLS), BF),
            pltpu.VMEM((4, 8, 128, BCOLS), BF),
            pltpu.VMEM((2 * ROWS, 512), F32),
            pltpu.VMEM((ROWS, 512), BF),
            pltpu.VMEM((ROWS, 512), BF),
            dma, dma((2,)), dma((2,)), dma((2,)), dma((3,)), dma((3,)), dma((3,)), dma((3,)),
            dma((u,)), dma((u,)), dma((u,)),
            dma((3,)), dma((3,)), dma((2, 4)), dma((2, 4)), dma((2, 4)), dma((2, 4)),
            dma((2, 8)), dma((2, 8)), dma((8,)), dma((8,)),
            dma((u, 2, 4)), dma((u, 2, 4)), dma((u, 8)), dma((u, 8)), dma, dma,
        ],
        compiler_params=pltpu.CompilerParams(
            collective_id=0, has_side_effects=True, vmem_limit_bytes=48 * 2**20
        ),
        cost_estimate=pl.CostEstimate(flops=flops, bytes_accessed=16 * 2**20, transcendentals=0),
        name="mixer",
    )(parts, out_weight, feat_taps, mixer_filter, skip_gain[None, :], meta, metac)
    return out, cost_out[0, 0:1]


def solution(mesh):
    placed = (
        P("ctx", None, "ch"),
        P("ctx"),
        P(None, None, "ch"),
        P("ch", None),
        P("ch"),
        P("ctx", "ch"),
        P("ctx"),
        P("ctx"),
    )
    return jax.shard_map(
        local, mesh=mesh, in_specs=placed, out_specs=(P("ctx", "ch"), P("ctx")), check_vma=False
    )
```

```python
import functools

import jax
import jax.numpy as jnp
from jax import lax
from jax.experimental import pallas as pl
from jax.experimental.pallas import tpu as pltpu
from jax.sharding import PartitionSpec as P

MESH = pl.DeviceIdType.MESH
BF = jnp.bfloat16
F32 = jnp.float32
ROWS = 160
TAPS = 128
UNITS = 2
ACOLS = 128
BCOLS = 384


def place():
    ctx = lax.axis_index("ctx")
    return ctx // 16, (ctx // 2) % 8, ctx % 2, lax.axis_index("ch"), ctx


def offset_of(j):
    return ((j + 1) // 2) * (2 * (j % 2) - 1)


def iota(shape, dim):
    return lax.broadcasted_iota(jnp.int32, shape, dim)


def mixer_kernel(
    feat_in, w_in, taps_in, filt_in, gain_in, seg_in, tgt_in, cost_in,
    out, cost_out,
    taps, filt, gain, seg_v, tgt_v, cost_v, meta, s_in, feat, qf, win, hrev, circ, mask_a, mask_b, gsend, gbuf, cbuf, slots, prevmeta,
    packed, arrived, abuf, wa, wb, acc, osend, orecv,
    s_feat, s_loc, s_sib, r_sib, s_halo, r_halo, s_gx, r_gx, s_rel, r_rel, s_self,
    s_ax, r_ax, s_ay, r_ay, s_by, r_by, s_bx, r_bx, s_bx2, r_bx2,
    s_z, r_z, s_c, r_c, s_o, r_o,
):
    x, y, k, z, ctx = place()
    chip = x * 8 + y
    kk = 1 - k

    def dev(dx=0, dy=0, dz=0, dk=0):
        return (
            (((x + dx + 4) % 4) * 8 + (y + dy + 8) % 8) * 2 + (k + dk) % 2,
            (z + dz + 8) % 8,
        )

    sibling = dev(dk=1)
    following = ((ctx + 1) % 64, z)
    previous = ((ctx + 63) % 64, z)
    pending = []

    def send(src, dst, ssem, rsem, to):
        c = pltpu.make_async_remote_copy(
            src_ref=src, dst_ref=dst, send_sem=ssem, recv_sem=rsem,
            device_id=to, device_id_type=MESH,
        )
        c.start()
        pending.append(c)

    def arrived_at(dst, ssem, rsem):
        pltpu.make_async_remote_copy(
            src_ref=dst, dst_ref=dst, send_sem=ssem, recv_sem=rsem,
            device_id=sibling, device_id_type=MESH,
        ).wait_recv()

    own_a = wa.at[y, x]
    own_b = wb.at[x, y]
    mine = pl.ds(pl.multiple_of(k * 64, 64), 64)

    def wcols(core, first, count):
        return w_in.at[:, pl.ds(pl.multiple_of(core * 512 + first, 128), count)]

    def start_weights():
        copies = (
            pltpu.make_async_copy(wcols(k, 0, ACOLS), own_a.at[mine], s_loc.at[0]),
            pltpu.make_async_copy(wcols(k, ACOLS, BCOLS), own_b.at[mine], s_loc.at[1]),
        )
        for c in copies:
            c.start()
        return copies

    load = pltpu.make_async_copy(feat_in, feat.at[:, pl.ds(16, ROWS)], s_feat)
    load.start()
    w_loads = start_weights()
    loads = [
        pltpu.make_async_copy(src, dst, s_in.at[n])
        for n, (src, dst) in enumerate(
            ((seg_in, seg_v), (tgt_in, tgt_v), (cost_in, cost_v),
             (taps_in, taps), (filt_in, filt), (gain_in, gain))
        )
    ]
    for c in loads:
        c.start()
    barrier = pltpu.get_barrier_semaphore()

    def greet(i, carry):
        other = (chip + i) % 32
        pl.semaphore_signal(barrier, inc=1, device_id=(other * 2 + k, z), device_id_type=MESH)
        return carry

    lax.fori_loop(1, 32, greet, 0)
    for to in (sibling, following, previous, dev(dz=1), dev(dz=-1)):
        pl.semaphore_signal(barrier, inc=1, device_id=to, device_id_type=MESH)

    for c in loads:
        c.wait()

    def row_of(ref, fill):
        return jnp.concatenate([ref[...].astype(F32), jnp.full((1, 96), fill, F32)], axis=1)

    seg_pad = row_of(seg_v, -7.0)
    meta[0:1, :] = seg_pad
    meta[1:2, :] = row_of(tgt_v, -7.0)
    meta[2:3, :] = row_of(cost_v, 0.0)
    meta[3:4, :] = pltpu.roll(seg_pad, 256 - 32, 1)
    meta[4:8, :] = jnp.zeros((4, 256), F32)
    metac = meta[...].T[0:ROWS]
    seg_col = metac[:, 0:1]
    tgt_col = metac[:, 1:2]
    cost_col = metac[:, 2:3]
    lag = iota((ROWS, 384), 0) + TAPS - iota((ROWS, 384), 1)
    in_reach = (lag >= 0) & (lag < TAPS)

    def same_segment(prev_row):
        seg_row = jnp.concatenate([prev_row, meta[0:1, :]], axis=1)
        return jnp.where(in_reach & (seg_col == seg_row), 1.0, 0.0)

    def featurize(index, center, match_one, match_two):
        return (
            taps[index, 0:1, :] * center
            + taps[index, 1:2, :] * pltpu.roll(center, 1, 0) * match_one
            + taps[index, 2:3, :] * pltpu.roll(center, 2, 0) * match_two
        )

    seg_own = same_segment(jnp.full((1, 128), -1.0, F32))
    back = jnp.sum(seg_own, axis=1, keepdims=True)
    m_one = jnp.where(back > 1.5, 1.0, 0.0)
    m_two = jnp.where(back > 2.5, 1.0, 0.0)
    load.wait()
    own_rows = pl.ds(16, ROWS)
    qf[...] = featurize(0, feat[0, own_rows].astype(F32), m_one, m_two)
    win[pl.ds(128, ROWS), :] = (
        featurize(1, feat[1, own_rows].astype(F32), m_one, m_two)
        * featurize(2, feat[2, own_rows].astype(F32), m_one, m_two)
    ).astype(BF)
    win[pl.ds(288, 96), :] = jnp.zeros((96, 512), BF)

    pl.semaphore_wait(barrier, 36)

    send(wcols(kk, 0, ACOLS), own_a.at[mine], s_sib.at[0], r_sib.at[0], sibling)
    send(wcols(kk, ACOLS, BCOLS), own_b.at[mine], s_sib.at[1], r_sib.at[1], sibling)
    send(feat.at[:, pl.ds(160, 16)], feat.at[:, pl.ds(0, 16)], s_halo.at[0], r_halo.at[0], following)
    send(meta, prevmeta, s_halo.at[1], r_halo.at[1], following)
    send(win.at[pl.ds(160, 128)], win.at[pl.ds(0, 128)], s_halo.at[2], r_halo.at[2], following)
    tgt_row = meta[1:2, :]
    same_target = tgt_col == tgt_row
    rq = iota((ROWS, 256), 0)
    rr = iota((ROWS, 256), 1)
    rank_row = jnp.sum(jnp.where(same_target & (rq < rr), 1.0, 0.0), axis=0, keepdims=True)
    rank_col = jnp.sum(jnp.where(same_target & (rr < rq), 1.0, 0.0), axis=1, keepdims=True)
    kf = k.astype(F32)
    mine_rows = pl.ds(pl.multiple_of(k * ROWS, 16), ROWS)
    chip_row = jnp.floor(tgt_row * 0.5)
    core_row = tgt_row - 2.0 * chip_row
    for u in range(UNITS):
        here = core_row == u
        slots[k, 2 * u:2 * u + 1, :] = jnp.where(here, chip_row * 16.0 + kf * 5.0 + rank_row, -1.0)
        slots[k, 2 * u + 1:2 * u + 2, :] = jnp.where(here, chip_row * 16.0 + 10.0, -1.0)
    slots[k, 4:8, :] = jnp.zeros((4, 256), F32)
    cbuf[mine_rows, :] = jnp.where(
        iota((ROWS, 128), 1).astype(F32) == kf * 5.0 + rank_col, cost_col, 0.0
    ).astype(BF)

    flip = (iota((TAPS, TAPS), 0) + iota((TAPS, TAPS), 1)) % TAPS == 0
    hrev[...] = jnp.dot(
        filt[...].astype(BF), jnp.where(flip, 1.0, 0.0).astype(BF), preferred_element_type=F32
    )

    send(slots.at[k], slots.at[k], s_gx.at[1], r_gx.at[1], sibling)
    send(cbuf.at[mine_rows], cbuf.at[mine_rows], s_gx.at[2], r_gx.at[2], sibling)

    def turn(i, carry):
        for n in range(4):
            row = jnp.broadcast_to(hrev[pl.ds(i * 4 + n, 1), :], (TAPS, TAPS))
            circ[i * 4 + n] = pltpu.roll(row, 0, 1, stride=1, stride_axis=0).astype(BF)
        return carry

    lax.fori_loop(0, 8, turn, 0)

    events = []

    def at(when, what, *args):
        events.append((when, len(events), functools.partial(what, *args)))

    def w_own():
        theirs = pl.ds(pl.multiple_of(kk * 64, 64), 64)
        for c in w_loads:
            c.wait()
        arrived_at(own_a.at[theirs], s_sib.at[0], r_sib.at[0])
        arrived_at(own_b.at[theirs], s_sib.at[1], r_sib.at[1])
        for d in (1, 2, 3):
            send(own_a, own_a, s_ax.at[d - 1], r_ax.at[d - 1], dev(dx=d))
        by_send(1)
        bx_send(0)

    def by_piece(t, way):
        ref = wb.at[x, (y + (1 - t if way == 0 else t - 1) + 8) % 8]
        return ref if t < 4 else ref.at[pl.ds(way * 64, 64)]

    def by_landed(t, way):
        ref = wb.at[x, (y + (-t if way == 0 else t) + 8) % 8]
        return ref if t < 4 else ref.at[pl.ds(way * 64, 64)]

    def by_send(t):
        for way in (0, 1):
            piece = by_piece(t, way)
            send(piece, piece, s_by.at[way, t - 1], r_by.at[way, t - 1], dev(dy=1 - 2 * way))

    def by_step(t):
        for way in (0, 1):
            arrived_at(by_landed(t, way), s_by.at[way, t - 1], r_by.at[way, t - 1])
        if t < 4:
            bx_send(2 * t - 1)
            bx_send(2 * t)
        else:
            bx_send(7)

    def ay_piece(t, way):
        ref = wa.at[(y + (1 - t if way == 0 else t - 1) + 8) % 8]
        return ref if t < 4 else ref.at[pl.ds(way * 2, 2)]

    def ay_landed(t, way):
        ref = wa.at[(y + (-t if way == 0 else t) + 8) % 8]
        return ref if t < 4 else ref.at[pl.ds(way * 2, 2)]

    def ay_send(t):
        for way in (0, 1):
            piece = ay_piece(t, way)
            send(piece, piece, s_ay.at[way, t - 1], r_ay.at[way, t - 1], dev(dy=1 - 2 * way))

    def ax_done():
        for d in (1, 2, 3):
            arrived_at(wa.at[y, (x - d + 4) % 4], s_ax.at[d - 1], r_ax.at[d - 1])
        ay_send(1)

    def ay_step(t):
        for way in (0, 1):
            arrived_at(ay_landed(t, way), s_ay.at[way, t - 1], r_ay.at[way, t - 1])
        if t < 4:
            ay_send(t + 1)

    def bx_row(j):
        return (y + offset_of(j) + 8) % 8

    def bx_send(j):
        piece = wb.at[x, bx_row(j)]
        for way in (0, 1):
            send(piece, piece, s_bx.at[way, j], r_bx.at[way, j], dev(dx=1 - 2 * way))

    def bx_step(j):
        for way in (0, 1):
            landed = wb.at[(x + 2 * way - 1 + 4) % 4, bx_row(j)]
            arrived_at(landed, s_bx.at[way, j], r_bx.at[way, j])
        way = j % 2
        piece = wb.at[(x + 2 * way - 1 + 4) % 4, bx_row(j)]
        send(piece, piece, s_bx2.at[j], r_bx2.at[j], dev(dx=1 - 2 * way))

    def w_last():
        for j in range(8):
            arrived_at(wb.at[(x + 2) % 4, bx_row(j)], s_bx2.at[j], r_bx2.at[j])

    def halo():
        arrived_at(prevmeta, s_halo.at[1], r_halo.at[1])
        arrived_at(feat.at[:, pl.ds(0, 16)], s_halo.at[0], r_halo.at[0])
        prev_row = jnp.where(ctx == 0, -1.0, prevmeta[3:4, 0:128])
        mask = same_segment(prev_row)
        mask_a[...] = mask[0:128, 0:256].astype(BF)
        mask_b[...] = mask[128:160, 128:384].astype(BF)
        count = jnp.sum(mask[0:32], axis=1, keepdims=True)[0:16]
        one = jnp.where(count > 1.5, 1.0, 0.0)
        two = jnp.where(count > 2.5, 1.0, 0.0)
        pad = jnp.zeros((16, 1), F32)
        one = jnp.concatenate([pad, one], axis=0)
        two = jnp.concatenate([pad, two], axis=0)
        fixed = [
            featurize(i, feat[i, pl.ds(0, 32)].astype(F32), one, two)[16:32] for i in range(3)
        ]
        qf[pl.ds(0, 16), :] = fixed[0]
        win[pl.ds(128, 16), :] = (fixed[1] * fixed[2]).astype(BF)
        arrived_at(win.at[pl.ds(0, 128)], s_halo.at[2], r_halo.at[2])

    def conv(part, dst, dst_rows):
        lane_group = iota((TAPS, 128), 1) // 16
        for tile in range(2):
            cols = pl.ds(pl.multiple_of(part * 256 + tile * 128, 128), 128)
            tall, low = [], []
            for n in range(8):
                turned = circ[part * 16 + tile * 8 + n]
                pair = jnp.concatenate([turned, turned], axis=1)
                tall.append(pair * mask_a[...])
                low.append(pair[0:32] * mask_b[...])
            res_a = jnp.dot(
                jnp.concatenate(tall, axis=0), win[pl.ds(0, 256), cols], preferred_element_type=F32
            )
            res_b = jnp.dot(
                jnp.concatenate(low, axis=0), win[pl.ds(128, 256), cols], preferred_element_type=F32
            )
            top, bottom = res_a[0:128], res_b[0:32]
            for n in range(1, 8):
                top = jnp.where(lane_group == n, res_a[n * 128:(n + 1) * 128], top)
                bottom = jnp.where(lane_group[0:32] == n, res_b[n * 32:(n + 1) * 32], bottom)
            total = jnp.concatenate([top, bottom], axis=0)
            center = win[pl.ds(128, ROWS), cols].astype(F32)
            dst[dst_rows, pl.ds(tile * 128, 128)] = (
                qf[:, cols] * (total + gain[:, cols] * center)
            ).astype(BF)

    def conv_theirs():
        conv(kk, gsend, pl.ds(0, ROWS))
        send(gsend, gbuf.at[mine_rows], s_gx.at[0], r_gx.at[0], sibling)

    def conv_mine():
        conv(k, gbuf, mine_rows)

    totals = []

    def unit_rows(u):
        return pl.ds(u * ROWS, ROWS)

    def pack(u):
        if u == 0:
            other_rows = pl.ds(pl.multiple_of(kk * ROWS, 16), ROWS)
            arrived_at(slots.at[kk], s_gx.at[1], r_gx.at[1])
            arrived_at(cbuf.at[other_rows], s_gx.at[2], r_gx.at[2])
            arrived_at(gbuf.at[other_rows], s_gx.at[0], r_gx.at[0])

        def pick(n):
            slot = jnp.concatenate([slots[0, n:n + 1, 0:ROWS], slots[1, n:n + 1, 0:ROWS]], axis=1)
            return jnp.where(iota((512, 2 * ROWS), 0).astype(F32) == slot, 1.0, 0.0).astype(BF)

        res = jnp.dot(pick(2 * u), gbuf[...], preferred_element_type=F32)
        costs = jnp.dot(pick(2 * u + 1), cbuf[...], preferred_element_type=F32)
        res = jnp.concatenate([res[:, 0:128] + costs, res[:, 128:256]], axis=1)
        packed[u] = res.astype(BF)

        block = pl.ds(pl.multiple_of(chip * 16, 16), 16)
        pltpu.make_async_copy(packed.at[u, block], arrived.at[u, block], s_self.at[u]).start()

        def post(i, carry):
            dx = i % 4
            dy = offset_of(i // 4)
            other = ((x + dx) % 4) * 8 + (y + dy + 8) % 8
            theirs = pl.ds(pl.multiple_of(other * 16, 16), 16)
            pltpu.make_async_remote_copy(
                src_ref=packed.at[u, theirs], dst_ref=arrived.at[u, block],
                send_sem=s_rel.at[u], recv_sem=r_rel.at[u],
                device_id=(other * 2 + k, z), device_id_type=MESH,
            ).start()
            return carry

        lax.fori_loop(1, 32, post, 0)

    def relay_wait(u):
        block = pl.ds(pl.multiple_of(chip * 16, 16), 16)
        bulk = pltpu.make_async_remote_copy(
            src_ref=packed.at[u, pl.ds(0, 496)], dst_ref=arrived.at[u, pl.ds(0, 496)],
            send_sem=s_rel.at[u], recv_sem=r_rel.at[u],
            device_id=sibling, device_id_type=MESH,
        )
        bulk.wait_send()
        bulk.wait_recv()
        pltpu.make_async_copy(packed.at[u, block], arrived.at[u, block], s_self.at[u]).wait()

    def unpack(u):
        relay_wait(u)
        pickc = jnp.where(iota((32, 512), 1) == iota((32, 512), 0) * 16 + 10, 1.0, 0.0)
        costs = jnp.dot(pickc.astype(BF), arrived[u, :, 0:128], preferred_element_type=F32)
        totals.append(jnp.sum(costs) / (32.0 * ROWS))
        live = jnp.where(costs > 0.5, 1.0, 0.0)
        a = iota((128, 128), 0)
        b = iota((128, 128), 1)
        both = (a % 5 == 0) & (a < 10) & (b < 10)
        first = (a == 0) & (b >= 5) & (b < 10)
        live_b = live.astype(BF)
        tally = jnp.dot(live_b, jnp.where(both, 1.0, 0.0).astype(BF), preferred_element_type=F32)
        before = jnp.dot(live_b, jnp.where(first, 1.0, 0.0).astype(BF), preferred_element_type=F32)
        lower = jnp.where(iota((32, 32), 1) < iota((32, 32), 0), 1.0, 0.0)
        rank = jnp.dot(lower.astype(BF), tally.astype(BF), preferred_element_type=F32) + before
        code = jnp.where(live > 0.5, rank + 1.0, 0.0)
        spread = jnp.where(iota((128, 512), 0) == iota((128, 512), 1) % 16, 1.0, 0.0)
        wide = jnp.dot(code.astype(BF), spread.astype(BF), preferred_element_type=F32)
        mine_only = iota((32, 512), 0) == iota((32, 512), 1) // 16
        code_row = jnp.sum(jnp.where(mine_only, wide, 0.0), axis=0, keepdims=True)
        i_row = iota((1, 512), 1) % 16
        dest = (i_row % 5).astype(F32) + 5.0 * (code_row - 1.0)
        dest = jnp.where((code_row > 0.5) & (i_row < 10), dest, -1.0)
        hit = jnp.where(iota((ROWS, 512), 0).astype(F32) == dest, 1.0, 0.0).astype(BF)
        rows = jnp.dot(hit, arrived[u], preferred_element_type=F32).astype(BF)
        abuf[z * 2 + k, unit_rows(u), :] = rows
        z_send(u, 1)
        mine_slot = abuf.at[z * 2 + k, unit_rows(u)]
        send(mine_slot, mine_slot, s_c.at[u, 0], r_c.at[u, 0], sibling)

    def z_slot(u, off, core):
        return abuf.at[((z + off + 8) % 8) * 2 + core, unit_rows(u)]

    def z_part(ref, t, way):
        return ref if t < 4 else ref.at[pl.ds(way * 80, 80)]

    def z_send(u, t):
        for way in (0, 1):
            piece = z_part(z_slot(u, 1 - t if way == 0 else t - 1, k), t, way)
            send(piece, piece, s_z.at[u, way, t - 1], r_z.at[u, way, t - 1], dev(dz=1 - 2 * way))

    def z_step(u, t):
        for way in (0, 1):
            landed = z_part(z_slot(u, -t if way == 0 else t, k), t, way)
            arrived_at(landed, s_z.at[u, way, t - 1], r_z.at[u, way, t - 1])
        if t < 4:
            z_send(u, t + 1)
        for j in ((2 * t - 1, 2 * t) if t < 4 else (7,)):
            piece = z_slot(u, offset_of(j), k)
            send(piece, piece, s_c.at[u, j], r_c.at[u, j], sibling)

    def multiply(first, last):
        def step(j, carry):
            zo = (z + offset_of(j) + 8) % 8
            for u in range(UNITS):
                arrived_at(abuf.at[zo * 2 + kk, unit_rows(u)], s_c.at[u, j], r_c.at[u, j])
            xs = zo // 2
            for half in (0, 1):
                ys = (zo % 2) * 4 + 2 * half
                part_a = jnp.concatenate([wa[ys, xs], wa[ys + 1, xs]], axis=0)
                part_b = jnp.concatenate([wb[xs, ys], wb[xs, ys + 1]], axis=0)
                weights = jnp.concatenate([part_a, part_b], axis=1)
                acc[...] += jnp.dot(
                    abuf[zo * 2 + half], weights, preferred_element_type=F32
                )
            return carry

        lax.fori_loop(first, last, step, 0)

    def clear():
        acc[...] = jnp.zeros_like(acc)

    def finish():
        theirs = pl.ds(pl.multiple_of(kk * ROWS, 16), ROWS)
        cost_out[0] = jnp.where(k == 0, totals[0], totals[1])
        osend[...] = acc[theirs, :].astype(BF)
        send(osend, orecv, s_o, r_o, sibling)
        out[:, pl.ds(pl.multiple_of(k * 512, 512), 512)] = acc[mine_rows, :].astype(BF)
        arrived_at(orecv, s_o, r_o)
        out[:, pl.ds(pl.multiple_of(kk * 512, 512), 512)] = orecv[...]

    plan = (
        (w_own, 1),
        (halo, 2),
        (conv_theirs, 3),
        (ax_done, 4),
        (by_step, 5, 1),
        (by_send, 6, 2),
        (conv_mine, 7),
        (pack, 8, 0),
        (pack, 9, 1),
        (clear, 10),
        (bx_step, 11, 0),
        (by_step, 12, 2),
        (bx_step, 13, 1),
        (bx_step, 14, 2),
        (unpack, 15, 0),
        (by_send, 16, 3),
        (unpack, 17, 1),
        (ay_step, 18, 1),
        (z_step, 19, 0, 1),
        (by_step, 20, 3),
        (by_send, 21, 4),
        (bx_step, 22, 3),
        (bx_step, 23, 4),
        (z_step, 24, 1, 1),
        (ay_step, 25, 2),
        (z_step, 26, 0, 2),
        (by_step, 27, 4),
        (bx_step, 28, 5),
        (z_step, 29, 1, 2),
        (bx_step, 30, 6),
        (ay_step, 31, 3),
        (z_step, 32, 0, 3),
        (bx_step, 33, 7),
        (z_step, 34, 1, 3),
        (ay_step, 35, 4),
        (w_last, 36),
        (multiply, 37, 0, 5),
        (z_step, 38, 0, 4),
        (z_step, 39, 1, 4),
        (multiply, 40, 5, 8),
        (finish, 41),
    )
    for what, when, *args in plan:
        at(when, what, *args)
    for _, _, run in sorted(events, key=lambda e: e[:2]):
        run()
    for c in pending:
        c.wait_send()


def local(features, segment_ids, feat_taps, mixer_filter, skip_gain, out_weight, targets, row_costs):
    parts = jnp.transpose(features, (1, 0, 2))
    vmem = pl.BlockSpec(memory_space=pltpu.VMEM)
    hbm = pl.BlockSpec(memory_space=pltpu.HBM)
    dma = pltpu.SemaphoreType.DMA
    u = UNITS
    flops = 2 * 320 * 4096 * 512
    out, cost_out = pl.pallas_call(
        mixer_kernel,
        out_shape=(
            jax.ShapeDtypeStruct((ROWS, 1024), BF),
            jax.ShapeDtypeStruct((1,), F32),
        ),
        in_specs=[hbm] * 8,
        out_specs=(vmem, pl.BlockSpec(memory_space=pltpu.SMEM)),
        scratch_shapes=[
            pltpu.VMEM((3, 3, 512), F32),
            pltpu.VMEM((32, TAPS), F32),
            pltpu.VMEM((1, 512), F32),
            pltpu.VMEM((1, ROWS), jnp.int32),
            pltpu.VMEM((1, ROWS), jnp.int32),
            pltpu.VMEM((1, ROWS), jnp.int32),
            pltpu.VMEM((8, 256), F32),
            dma((6,)),
            pltpu.VMEM((3, 16 + ROWS, 512), BF),
            pltpu.VMEM((ROWS, 512), F32),
            pltpu.VMEM((384, 512), BF),
            pltpu.VMEM((32, 128), F32),
            pltpu.VMEM((32, TAPS, TAPS), BF),
            pltpu.VMEM((128, 256), BF),
            pltpu.VMEM((32, 256), BF),
            pltpu.VMEM((ROWS, 256), BF),
            pltpu.VMEM((2 * ROWS, 256), BF),
            pltpu.VMEM((2 * ROWS, 128), BF),
            pltpu.VMEM((2, 8, 256), F32),
            pltpu.VMEM((8, 256), F32),
            pltpu.VMEM((u, 512, 256), BF),
            pltpu.VMEM((u, 512, 256), BF),
            pltpu.VMEM((16, 2 * ROWS, 256), BF),
            pltpu.VMEM((8, 4, 128, ACOLS), BF),
            pltpu.VMEM((4, 8, 128, BCOLS), BF),
            pltpu.VMEM((2 * ROWS, 512), F32),
            pltpu.VMEM((ROWS, 512), BF),
            pltpu.VMEM((ROWS, 512), BF),
            dma, dma((2,)), dma((2,)), dma((2,)), dma((3,)), dma((3,)), dma((3,)), dma((3,)),
            dma((u,)), dma((u,)), dma((u,)),
            dma((3,)), dma((3,)), dma((2, 4)), dma((2, 4)), dma((2, 4)), dma((2, 4)),
            dma((2, 8)), dma((2, 8)), dma((8,)), dma((8,)),
            dma((u, 2, 4)), dma((u, 2, 4)), dma((u, 8)), dma((u, 8)), dma, dma,
        ],
        compiler_params=pltpu.CompilerParams(
            collective_id=0, has_side_effects=True, vmem_limit_bytes=60 * 2**20
        ),
        cost_estimate=pl.CostEstimate(flops=flops, bytes_accessed=16 * 2**20, transcendentals=0),
        name="mixer",
    )(
        parts, out_weight, feat_taps, mixer_filter, skip_gain[None, :],
        segment_ids[None, :], targets[None, :], row_costs[None, :],
    )
    return out, cost_out


def solution(mesh):
    placed = (
        P("ctx", None, "ch"),
        P("ctx"),
        P(None, None, "ch"),
        P("ch", None),
        P("ch"),
        P("ctx", "ch"),
        P("ctx"),
        P("ctx"),
    )
    return jax.shard_map(
        local, mesh=mesh, in_specs=placed, out_specs=(P("ctx", "ch"), P("ctx")), check_vma=False
    )
```

```python
import functools

import jax
import jax.numpy as jnp
from jax import lax
from jax.experimental import pallas as pl
from jax.experimental.pallas import tpu as pltpu
from jax.sharding import PartitionSpec as P

MESH = pl.DeviceIdType.MESH
BF = jnp.bfloat16
F32 = jnp.float32
ROWS = 160
TAPS = 128
UNITS = 4
UNIT_ROWS = 80
ACOLS = 128
BCOLS = 384


def place():
    ctx = lax.axis_index("ctx")
    return ctx // 16, (ctx // 2) % 8, ctx % 2, lax.axis_index("ch"), ctx


def offset_of(j):
    return ((j + 1) // 2) * (2 * (j % 2) - 1)


def iota(shape, dim):
    return lax.broadcasted_iota(jnp.int32, shape, dim)


def mixer_kernel(
    feat_in, w_in, taps_in, filt_in, gain_in, seg_in, tgt_in, cost_in,
    out, cost_out,
    taps, filt, gain, seg_v, tgt_v, cost_v, meta, s_in, feat, qf, win, hrev, circ, mask_a, mask_b, gsend, gbuf, cbuf, slots, prevmeta,
    packed, arrived, abuf, wa, wb, acc, osend, okeep,
    s_feat, s_loc, s_sib, r_sib, s_halo, r_halo, s_gx, r_gx, s_rel, r_rel, s_self,
    s_ax, r_ax, s_ay, r_ay, s_by, r_by, s_bx, r_bx, s_bx2, r_bx2,
    s_z, r_z, s_c, r_c, s_o, r_o, s_keep,
):
    x, y, k, z, ctx = place()
    chip = x * 8 + y
    kk = 1 - k

    def dev(dx=0, dy=0, dz=0, dk=0):
        return (
            (((x + dx + 4) % 4) * 8 + (y + dy + 8) % 8) * 2 + (k + dk) % 2,
            (z + dz + 8) % 8,
        )

    sibling = dev(dk=1)
    following = ((ctx + 1) % 64, z)
    previous = ((ctx + 63) % 64, z)
    pending = []

    def send(src, dst, ssem, rsem, to):
        c = pltpu.make_async_remote_copy(
            src_ref=src, dst_ref=dst, send_sem=ssem, recv_sem=rsem,
            device_id=to, device_id_type=MESH,
        )
        c.start()
        pending.append(c)

    def arrived_at(dst, ssem, rsem):
        pltpu.make_async_remote_copy(
            src_ref=dst, dst_ref=dst, send_sem=ssem, recv_sem=rsem,
            device_id=sibling, device_id_type=MESH,
        ).wait_recv()

    own_a = wa.at[y, x]
    own_b = wb.at[x, y]
    mine = pl.ds(pl.multiple_of(k * 64, 64), 64)

    def wcols(core, first, count):
        return w_in.at[:, pl.ds(pl.multiple_of(core * 512 + first, 128), count)]

    def start_weights():
        copies = (
            pltpu.make_async_copy(wcols(k, 0, ACOLS), own_a.at[mine], s_loc.at[0]),
            pltpu.make_async_copy(wcols(k, ACOLS, BCOLS), own_b.at[mine], s_loc.at[1]),
        )
        for c in copies:
            c.start()
        return copies

    load = pltpu.make_async_copy(feat_in, feat.at[:, pl.ds(16, ROWS)], s_feat)
    load.start()
    w_loads = start_weights()
    loads = [
        pltpu.make_async_copy(src, dst, s_in.at[n])
        for n, (src, dst) in enumerate(
            ((seg_in, seg_v), (tgt_in, tgt_v), (cost_in, cost_v),
             (taps_in, taps), (filt_in, filt), (gain_in, gain))
        )
    ]
    for c in loads:
        c.start()
    barrier = pltpu.get_barrier_semaphore()

    def greet(i, carry):
        other = (chip + i) % 32
        pl.semaphore_signal(barrier, inc=1, device_id=(other * 2 + k, z), device_id_type=MESH)
        return carry

    lax.fori_loop(1, 32, greet, 0)
    for to in (sibling, following, previous, dev(dz=1), dev(dz=-1)):
        pl.semaphore_signal(barrier, inc=1, device_id=to, device_id_type=MESH)

    for c in loads:
        c.wait()

    def row_of(ref, fill):
        return jnp.concatenate([ref[...].astype(F32), jnp.full((1, 96), fill, F32)], axis=1)

    seg_pad = row_of(seg_v, -7.0)
    meta[0:1, :] = seg_pad
    meta[1:2, :] = row_of(tgt_v, -7.0)
    meta[2:3, :] = row_of(cost_v, 0.0)
    meta[3:4, :] = pltpu.roll(seg_pad, 256 - 32, 1)
    meta[4:8, :] = jnp.zeros((4, 256), F32)
    metac = meta[...].T[0:ROWS]
    seg_col = metac[:, 0:1]
    tgt_col = metac[:, 1:2]
    cost_col = metac[:, 2:3]
    lag = iota((ROWS, 384), 0) + TAPS - iota((ROWS, 384), 1)
    in_reach = (lag >= 0) & (lag < TAPS)

    def same_segment(prev_row):
        seg_row = jnp.concatenate([prev_row, meta[0:1, :]], axis=1)
        return jnp.where(in_reach & (seg_col == seg_row), 1.0, 0.0)

    def featurize(index, center, match_one, match_two):
        return (
            taps[index, 0:1, :] * center
            + taps[index, 1:2, :] * pltpu.roll(center, 1, 0) * match_one
            + taps[index, 2:3, :] * pltpu.roll(center, 2, 0) * match_two
        )

    seg_own = same_segment(jnp.full((1, 128), -1.0, F32))
    back = jnp.sum(seg_own, axis=1, keepdims=True)
    m_one = jnp.where(back > 1.5, 1.0, 0.0)
    m_two = jnp.where(back > 2.5, 1.0, 0.0)
    load.wait()
    own_rows = pl.ds(16, ROWS)
    qf[...] = featurize(0, feat[0, own_rows].astype(F32), m_one, m_two)
    win[pl.ds(128, ROWS), :] = (
        featurize(1, feat[1, own_rows].astype(F32), m_one, m_two)
        * featurize(2, feat[2, own_rows].astype(F32), m_one, m_two)
    ).astype(BF)
    win[pl.ds(288, 96), :] = jnp.zeros((96, 512), BF)

    mine_rows = pl.ds(pl.multiple_of(k * ROWS, 16), ROWS)
    pl.semaphore_wait(barrier, 36)

    send(wcols(kk, 0, ACOLS), own_a.at[mine], s_sib.at[0], r_sib.at[0], sibling)
    send(wcols(kk, ACOLS, BCOLS), own_b.at[mine], s_sib.at[1], r_sib.at[1], sibling)
    send(feat.at[:, pl.ds(160, 16)], feat.at[:, pl.ds(0, 16)], s_halo.at[0], r_halo.at[0], following)
    send(meta, prevmeta, s_halo.at[1], r_halo.at[1], following)
    send(win.at[pl.ds(160, 128)], win.at[pl.ds(0, 128)], s_halo.at[2], r_halo.at[2], following)
    events = []

    def at(when, what, *args):
        events.append((when, len(events), functools.partial(what, *args)))

    def ranks():
        tgt_row = meta[1:2, :]
        same_target = tgt_col == tgt_row
        rq = iota((ROWS, 256), 0)
        rr = iota((ROWS, 256), 1)
        rank_row = jnp.sum(jnp.where(same_target & (rq < rr), 1.0, 0.0), axis=0, keepdims=True)
        rank_col = jnp.sum(jnp.where(same_target & (rr < rq), 1.0, 0.0), axis=1, keepdims=True)
        kf = k.astype(F32)
        chip_row = jnp.floor(tgt_row * 0.5)
        chip_col = jnp.floor(tgt_col * 0.5)
        i_row = (tgt_row - 2.0 * chip_row) * 10.0 + kf * 5.0 + rank_row
        i_col = (tgt_col - 2.0 * chip_col) * 10.0 + kf * 5.0 + rank_col
        first = chip_row * 16.0
        slots[k, 0:1, :] = jnp.where(i_row < 15.5, first + i_row, -1.0)
        slots[k, 1:2, :] = jnp.where(i_row > 15.5, first + i_row - 16.0, -1.0)
        slots[k, 2:3, :] = jnp.where(i_row > 15.5, first + i_row - 12.0, -1.0)
        slots[k, 3:4, :] = first + 8.0
        slots[k, 4:8, :] = jnp.zeros((4, 256), F32)
        cbuf[mine_rows, :] = jnp.where(
            iota((ROWS, 128), 1).astype(F32) == i_col, cost_col, 0.0
        ).astype(BF)
        send(slots.at[k], slots.at[k], s_gx.at[1], r_gx.at[1], sibling)
        send(cbuf.at[mine_rows], cbuf.at[mine_rows], s_gx.at[2], r_gx.at[2], sibling)

    def filters():
        flip = (iota((TAPS, TAPS), 0) + iota((TAPS, TAPS), 1)) % TAPS == 0
        hrev[...] = jnp.dot(
            filt[...].astype(BF), jnp.where(flip, 1.0, 0.0).astype(BF), preferred_element_type=F32
        )

        def turn(i, carry):
            for n in range(4):
                row = jnp.broadcast_to(hrev[pl.ds(i * 4 + n, 1), :], (TAPS, TAPS))
                circ[i * 4 + n] = pltpu.roll(row, 0, 1, stride=1, stride_axis=0).astype(BF)
            return carry

        lax.fori_loop(0, 8, turn, 0)

    def w_own():
        theirs = pl.ds(pl.multiple_of(kk * 64, 64), 64)
        for c in w_loads:
            c.wait()
        arrived_at(own_a.at[theirs], s_sib.at[0], r_sib.at[0])
        arrived_at(own_b.at[theirs], s_sib.at[1], r_sib.at[1])
        for d in (1, 2, 3):
            send(own_a, own_a, s_ax.at[d - 1], r_ax.at[d - 1], dev(dx=d))
        by_send(1)
        bx_send(0)

    def by_piece(t, way):
        ref = wb.at[x, (y + (1 - t if way == 0 else t - 1) + 8) % 8]
        return ref if t < 4 else ref.at[pl.ds(way * 64, 64)]

    def by_landed(t, way):
        ref = wb.at[x, (y + (-t if way == 0 else t) + 8) % 8]
        return ref if t < 4 else ref.at[pl.ds(way * 64, 64)]

    def by_send(t):
        for way in (0, 1):
            piece = by_piece(t, way)
            send(piece, piece, s_by.at[way, t - 1], r_by.at[way, t - 1], dev(dy=1 - 2 * way))

    def by_step(t):
        for way in (0, 1):
            arrived_at(by_landed(t, way), s_by.at[way, t - 1], r_by.at[way, t - 1])
        if t < 4:
            bx_send(2 * t - 1)
            bx_send(2 * t)
        else:
            bx_send(7)

    def ay_part(off, h):
        return wa.at[(y + off + 8) % 8, pl.ds(2 * h, 2)]

    def ay_ways(t, h):
        return (0, 1) if t < 4 else (h,)

    def ay_send(t, h):
        for way in ay_ways(t, h):
            piece = ay_part(1 - t if way == 0 else t - 1, h)
            send(
                piece, piece, s_ay.at[way, t - 1, h], r_ay.at[way, t - 1, h], dev(dy=1 - 2 * way)
            )

    def ax_done():
        for d in (1, 2, 3):
            arrived_at(wa.at[y, (x - d + 4) % 4], s_ax.at[d - 1], r_ax.at[d - 1])
        for h in (0, 1):
            ay_send(1, h)

    def ay_step(t):
        for h in (0, 1):
            for way in ay_ways(t, h):
                landed = ay_part(-t if way == 0 else t, h)
                arrived_at(landed, s_ay.at[way, t - 1, h], r_ay.at[way, t - 1, h])
            if t < 4:
                ay_send(t + 1, h)

    def bx_row(j):
        return (y + offset_of(j) + 8) % 8

    def bx_send(j):
        piece = wb.at[x, bx_row(j)]
        for way in (0, 1):
            send(piece, piece, s_bx.at[way, j], r_bx.at[way, j], dev(dx=1 - 2 * way))

    def bx_step(j):
        for way in (0, 1):
            landed = wb.at[(x + 2 * way - 1 + 4) % 4, bx_row(j)]
            arrived_at(landed, s_bx.at[way, j], r_bx.at[way, j])
        way = j % 2
        piece = wb.at[(x + 2 * way - 1 + 4) % 4, bx_row(j)]
        send(piece, piece, s_bx2.at[j], r_bx2.at[j], dev(dx=1 - 2 * way))

    def w_last():
        for j in range(8):
            arrived_at(wb.at[(x + 2) % 4, bx_row(j)], s_bx2.at[j], r_bx2.at[j])

    def halo():
        arrived_at(prevmeta, s_halo.at[1], r_halo.at[1])
        arrived_at(feat.at[:, pl.ds(0, 16)], s_halo.at[0], r_halo.at[0])
        prev_row = jnp.where(ctx == 0, -1.0, prevmeta[3:4, 0:128])
        mask = same_segment(prev_row)
        mask_a[...] = mask[0:128, 0:256].astype(BF)
        mask_b[...] = mask[128:160, 128:384].astype(BF)
        count = jnp.sum(mask[0:32], axis=1, keepdims=True)[0:16]
        one = jnp.where(count > 1.5, 1.0, 0.0)
        two = jnp.where(count > 2.5, 1.0, 0.0)
        pad = jnp.zeros((16, 1), F32)
        one = jnp.concatenate([pad, one], axis=0)
        two = jnp.concatenate([pad, two], axis=0)
        fixed = [
            featurize(i, feat[i, pl.ds(0, 32)].astype(F32), one, two)[16:32] for i in range(3)
        ]
        qf[pl.ds(0, 16), :] = fixed[0]
        win[pl.ds(128, 16), :] = (fixed[1] * fixed[2]).astype(BF)
        arrived_at(win.at[pl.ds(0, 128)], s_halo.at[2], r_halo.at[2])

    def conv(part, dst, dst_rows):
        lane_group = iota((TAPS, 128), 1) // 16
        for tile in range(2):
            cols = pl.ds(pl.multiple_of(part * 256 + tile * 128, 128), 128)
            tall, low = [], []
            for n in range(8):
                turned = circ[part * 16 + tile * 8 + n]
                pair = jnp.concatenate([turned, turned], axis=1)
                tall.append(pair * mask_a[...])
                low.append(pair[0:32] * mask_b[...])
            res_a = jnp.dot(
                jnp.concatenate(tall, axis=0), win[pl.ds(0, 256), cols], preferred_element_type=F32
            )
            res_b = jnp.dot(
                jnp.concatenate(low, axis=0), win[pl.ds(128, 256), cols], preferred_element_type=F32
            )
            top, bottom = res_a[0:128], res_b[0:32]
            for n in range(1, 8):
                top = jnp.where(lane_group == n, res_a[n * 128:(n + 1) * 128], top)
                bottom = jnp.where(lane_group[0:32] == n, res_b[n * 32:(n + 1) * 32], bottom)
            total = jnp.concatenate([top, bottom], axis=0)
            center = win[pl.ds(128, ROWS), cols].astype(F32)
            dst[dst_rows, pl.ds(tile * 128, 128)] = (
                qf[:, cols] * (total + gain[:, cols] * center)
            ).astype(BF)

    def conv_theirs():
        conv(kk, gsend, pl.ds(0, ROWS))
        send(gsend, gbuf.at[mine_rows], s_gx.at[0], r_gx.at[0], sibling)

    def conv_mine():
        conv(k, gbuf, mine_rows)

    def unit_rows(u):
        return pl.ds(u * UNIT_ROWS, UNIT_ROWS)

    own_block = pl.ds(pl.multiple_of(chip * 16, 16), 16)

    def keep_own():
        return pltpu.make_async_copy(packed.at[own_block], arrived.at[own_block], s_self)

    def pack():
        other_rows = pl.ds(pl.multiple_of(kk * ROWS, 16), ROWS)
        arrived_at(slots.at[kk], s_gx.at[1], r_gx.at[1])
        arrived_at(cbuf.at[other_rows], s_gx.at[2], r_gx.at[2])
        place_row = iota((512, 2 * ROWS), 0).astype(F32)

        def pick(n):
            slot = jnp.concatenate([slots[0, n:n + 1, 0:ROWS], slots[1, n:n + 1, 0:ROWS]], axis=1)
            return jnp.where(place_row == slot, 1.0, 0.0).astype(BF)

        arrived_at(gbuf.at[other_rows], s_gx.at[0], r_gx.at[0])
        packed[:, 0:256] = jnp.dot(pick(0), gbuf[...], preferred_element_type=F32).astype(BF)
        packed[:, 256:384] = (
            jnp.dot(pick(1), gbuf[:, 0:128], preferred_element_type=F32)
            + jnp.dot(pick(2), gbuf[:, 128:256], preferred_element_type=F32)
            + jnp.dot(pick(3), cbuf[...], preferred_element_type=F32)
        ).astype(BF)
        keep_own().start()

        def post(i, carry):
            other = ((x + i // 8 + i % 8) % 4) * 8 + (y + offset_of(7 - i % 8) + 8) % 8
            pltpu.make_async_remote_copy(
                src_ref=packed.at[pl.ds(pl.multiple_of(other * 16, 16), 16)],
                dst_ref=arrived.at[own_block], send_sem=s_rel, recv_sem=r_rel,
                device_id=(other * 2 + k, z), device_id_type=MESH,
            ).start()
            return carry

        lax.fori_loop(0, 15, post, 0)
        lax.fori_loop(16, 32, post, 0)

    def relay_wait():
        bulk = pltpu.make_async_remote_copy(
            src_ref=packed.at[pl.ds(0, 496)], dst_ref=arrived.at[pl.ds(0, 496)],
            send_sem=s_rel, recv_sem=r_rel, device_id=sibling, device_id_type=MESH,
        )
        bulk.wait_send()
        bulk.wait_recv()
        keep_own().wait()

    def unpack():
        col = iota((1, 512), 1) % 16
        spread_i = iota((128, 512), 0)
        spread_c = iota((128, 512), 1) % 16
        spread_a = jnp.where(spread_i == spread_c, 1.0, 0.0).astype(BF)
        spread_b = jnp.where((spread_c < 8) & (spread_i == 16 + spread_c % 4), 1.0, 0.0).astype(BF)
        mine_only = iota((32, 512), 0) == iota((32, 512), 1) // 16
        pickc = jnp.where(iota((32, 512), 1) == iota((32, 512), 0) * 16 + 8, 1.0, 0.0).astype(BF)
        a = iota((128, 128), 0)
        b = iota((128, 128), 1)
        both = (a // 10 == b // 10) & (a % 5 == 0) & (b < 20)
        first = both & (a % 10 == 0) & (b % 10 >= 5)
        both = jnp.where(both, 1.0, 0.0).astype(BF)
        first = jnp.where(first, 1.0, 0.0).astype(BF)
        lower = jnp.where(iota((32, 32), 1) < iota((32, 32), 0), 1.0, 0.0).astype(BF)
        lane = iota((32, 128), 1)
        relay_wait()
        costs = jnp.dot(pickc, arrived[:, 256:384], preferred_element_type=F32)
        mine_lane = (lane >= k * 10) & (lane < k * 10 + 10)
        cost_out[0] = jnp.sum(jnp.where(mine_lane, costs, 0.0)) / (32.0 * ROWS)
        live = jnp.where(costs > 0.5, 1.0, 0.0).astype(BF)
        tally = jnp.dot(live, both, preferred_element_type=F32)
        before = jnp.dot(live, first, preferred_element_type=F32)
        rank = jnp.dot(lower, tally.astype(BF), preferred_element_type=F32) + before
        code = jnp.where(costs > 0.5, rank + 1.0, 0.0).astype(BF)

        def dest_row(spread, i):
            wide = jnp.dot(code, spread, preferred_element_type=F32)
            code_row = jnp.sum(jnp.where(mine_only, wide, 0.0), axis=0, keepdims=True)
            dest = ((i // 10) * ROWS + i % 5).astype(F32) + 5.0 * (code_row - 1.0)
            return jnp.where(code_row > 0.5, dest, -1.0)

        dest_a = dest_row(spread_a, col)
        dest_b = dest_row(spread_b, 16 + col % 4)
        dest_lo = jnp.where(col < 4, dest_b, -1.0)
        dest_hi = jnp.where(col >= 4, dest_b, -1.0)
        target = iota((ROWS, 512), 0).astype(F32)
        for part in range(2):

            def hit(dest):
                return jnp.where(target == dest - float(part * ROWS), 1.0, 0.0).astype(BF)

            main = jnp.dot(hit(dest_a), arrived[:, 0:256], preferred_element_type=F32)
            low = jnp.dot(hit(dest_lo), arrived[:, 256:384], preferred_element_type=F32)
            high = jnp.dot(hit(dest_hi), arrived[:, 256:384], preferred_element_type=F32)
            rows = jnp.concatenate([main[:, 0:128] + low, main[:, 128:256] + high], axis=1)
            abuf[z * 2 + k, pl.ds(part * ROWS, ROWS), :] = rows.astype(BF)
            for u in (2 * part, 2 * part + 1):
                z_send(u, 1)
        for u in range(UNITS):
            mine_slot = abuf.at[z * 2 + k, unit_rows(u)]
            send(mine_slot, mine_slot, s_c.at[u, 0], r_c.at[u, 0], sibling)

    def z_slot(u, off, core):
        return abuf.at[((z + off + 8) % 8) * 2 + core, unit_rows(u)]

    def z_ways(u, t):
        return (0, 1) if t < 4 else (u // 2,)

    def z_send(u, t):
        for way in z_ways(u, t):
            piece = z_slot(u, 1 - t if way == 0 else t - 1, k)
            send(piece, piece, s_z.at[u, way, t - 1], r_z.at[u, way, t - 1], dev(dz=1 - 2 * way))

    def z_step(t, *units):
        for u in units:
            for way in z_ways(u, t):
                landed = z_slot(u, -t if way == 0 else t, k)
                arrived_at(landed, s_z.at[u, way, t - 1], r_z.at[u, way, t - 1])
            if t < 4:
                z_send(u, t + 1)
            for j in ((2 * t - 1, 2 * t) if t < 4 else (7,)):
                piece = z_slot(u, offset_of(j), k)
                send(piece, piece, s_c.at[u, j], r_c.at[u, j], sibling)

    def multiply(first, last):
        def step(i, carry):
            rows, weights = [], []
            for n in range(2):
                j = 2 * i + n
                zo = (z + offset_of(j) + 8) % 8
                for u in range(UNITS):
                    arrived_at(abuf.at[zo * 2 + kk, unit_rows(u)], s_c.at[u, j], r_c.at[u, j])
                xs = zo // 2
                for half in (0, 1):
                    rows.append(abuf[zo * 2 + half])
                    for m in (0, 1):
                        ys = (zo % 2) * 4 + 2 * half + m
                        weights.append(jnp.concatenate([wa[ys, xs], wb[xs, ys]], axis=1))
            acc[...] += jnp.dot(
                jnp.concatenate(rows, axis=1), jnp.concatenate(weights, axis=0),
                preferred_element_type=F32,
            )
            return carry

        lax.fori_loop(first, last, step, 0)

    def clear():
        acc[...] = jnp.zeros_like(acc)

    def finish():
        cols = pl.ds(pl.multiple_of(k * 512, 512), 512)
        theirs = pl.ds(pl.multiple_of(kk * ROWS, 16), ROWS)
        osend[...] = acc[theirs, :].astype(BF)
        send(osend, out.at[:, cols], s_o, r_o, sibling)
        okeep[...] = acc[mine_rows, :].astype(BF)
        keep = pltpu.make_async_copy(okeep, out.at[:, cols], s_keep)
        keep.start()
        keep.wait()
        arrived_at(out.at[:, pl.ds(pl.multiple_of(kk * 512, 512), 512)], s_o, r_o)

    plan = (
        (w_own, 1),
        (ranks, 2),
        (filters, 3),
        (halo, 4),
        (conv_theirs, 5),
        (conv_mine, 6),
        (by_step, 7, 1),
        (by_send, 8, 2),
        (pack, 9),
        (ax_done, 10),
        (bx_step, 11, 0),
        (by_step, 12, 2),
        (by_send, 13, 3),
        (bx_step, 14, 1),
        (bx_step, 15, 2),
        (clear, 16),
        (unpack, 17),
        (bx_step, 18, 3),
        (bx_step, 19, 4),
        (ay_step, 20, 1),
        (by_step, 21, 3),
        (by_send, 22, 4),
        (z_step, 23, 1, 0, 1),
        (z_step, 24, 1, 2, 3),
        (ay_step, 25, 2),
        (by_step, 26, 4),
        (bx_step, 27, 5),
        (bx_step, 28, 6),
        (z_step, 29, 2, 0, 1),
        (z_step, 30, 2, 2, 3),
        (ay_step, 31, 3),
        (bx_step, 32, 7),
        (z_step, 33, 3, 0, 1),
        (z_step, 34, 3, 2, 3),
        (z_step, 35, 4, 0, 1),
        (z_step, 36, 4, 2, 3),
        (ay_step, 37, 4),
        (w_last, 38),
        (multiply, 39, 0, 4),
        (finish, 40),
    )
    for what, when, *args in plan:
        at(when, what, *args)
    for _, _, run in sorted(events, key=lambda e: e[:2]):
        run()
    for c in pending:
        c.wait_send()


def local(features, segment_ids, feat_taps, mixer_filter, skip_gain, out_weight, targets, row_costs):
    parts = jnp.transpose(features, (1, 0, 2))
    vmem = pl.BlockSpec(memory_space=pltpu.VMEM)
    hbm = pl.BlockSpec(memory_space=pltpu.HBM)
    dma = pltpu.SemaphoreType.DMA
    u = UNITS
    flops = 2 * 320 * 4096 * 512
    out, cost_out = pl.pallas_call(
        mixer_kernel,
        out_shape=(
            jax.ShapeDtypeStruct((ROWS, 1024), BF),
            jax.ShapeDtypeStruct((1,), F32),
        ),
        in_specs=[hbm] * 8,
        out_specs=(hbm, pl.BlockSpec(memory_space=pltpu.SMEM)),
        scratch_shapes=[
            pltpu.VMEM((3, 3, 512), F32),
            pltpu.VMEM((32, TAPS), F32),
            pltpu.VMEM((1, 512), F32),
            pltpu.VMEM((1, ROWS), jnp.int32),
            pltpu.VMEM((1, ROWS), jnp.int32),
            pltpu.VMEM((1, ROWS), jnp.int32),
            pltpu.VMEM((8, 256), F32),
            dma((6,)),
            pltpu.VMEM((3, 16 + ROWS, 512), BF),
            pltpu.VMEM((ROWS, 512), F32),
            pltpu.VMEM((384, 512), BF),
            pltpu.VMEM((32, 128), F32),
            pltpu.VMEM((32, TAPS, TAPS), BF),
            pltpu.VMEM((128, 256), BF),
            pltpu.VMEM((32, 256), BF),
            pltpu.VMEM((ROWS, 256), BF),
            pltpu.VMEM((2 * ROWS, 256), BF),
            pltpu.VMEM((2 * ROWS, 128), BF),
            pltpu.VMEM((2, 8, 256), F32),
            pltpu.VMEM((8, 256), F32),
            pltpu.VMEM((512, 384), BF),
            pltpu.VMEM((512, 384), BF),
            pltpu.VMEM((16, 2 * ROWS, 256), BF),
            pltpu.VMEM((8, 4, 128, ACOLS), BF),
            pltpu.VMEM((4, 8, 128, BCOLS), BF),
            pltpu.VMEM((2 * ROWS, 512), F32),
            pltpu.VMEM((ROWS, 512), BF),
            pltpu.VMEM((ROWS, 512), BF),
            dma, dma((2,)), dma((2,)), dma((2,)), dma((3,)), dma((3,)), dma((3,)), dma((3,)),
            dma, dma, dma,
            dma((3,)), dma((3,)), dma((2, 4, 2)), dma((2, 4, 2)), dma((2, 4)), dma((2, 4)),
            dma((2, 8)), dma((2, 8)), dma((8,)), dma((8,)),
            dma((u, 2, 4)), dma((u, 2, 4)), dma((u, 8)), dma((u, 8)), dma, dma, dma,
        ],
        compiler_params=pltpu.CompilerParams(
            collective_id=0, has_side_effects=True, vmem_limit_bytes=60 * 2**20
        ),
        cost_estimate=pl.CostEstimate(flops=flops, bytes_accessed=16 * 2**20, transcendentals=0),
        name="mixer",
    )(
        parts, out_weight, feat_taps, mixer_filter, skip_gain[None, :],
        segment_ids[None, :], targets[None, :], row_costs[None, :],
    )
    return out, cost_out


def solution(mesh):
    placed = (
        P("ctx", None, "ch"),
        P("ctx"),
        P(None, None, "ch"),
        P("ch", None),
        P("ch"),
        P("ctx", "ch"),
        P("ctx"),
        P("ctx"),
    )
    return jax.shard_map(
        local, mesh=mesh, in_specs=placed, out_specs=(P("ctx", "ch"), P("ctx")), check_vma=False
    )
```

```python
import functools

import jax
import jax.numpy as jnp
from jax import lax
from jax.experimental import pallas as pl
from jax.experimental.pallas import tpu as pltpu
from jax.sharding import PartitionSpec as P

MESH = pl.DeviceIdType.MESH
BF = jnp.bfloat16
F32 = jnp.float32
ROWS = 160
TAPS = 128
UNITS = 4
UNIT_ROWS = 80
ACOLS = 128
BCOLS = 384


def place():
    ctx = lax.axis_index("ctx")
    return ctx // 16, (ctx // 2) % 8, ctx % 2, lax.axis_index("ch"), ctx


def offset_of(j):
    return ((j + 1) // 2) * (2 * (j % 2) - 1)


def iota(shape, dim):
    return lax.broadcasted_iota(jnp.int32, shape, dim)


def mixer_kernel(
    feat_in, w_in, taps_in, filt_in, gain_in, seg_in, tgt_in, cost_in,
    out, cost_out,
    taps, filt, gain, seg_v, tgt_v, cost_v, meta, s_in, feat, qf, win, hrev, circ, mask_a, mask_b, gsend, gbuf, cbuf, slots, prevmeta,
    packed, arrived, abuf, wa, wb, acc, osend, okeep,
    s_feat, s_loc, s_sib, r_sib, s_halo, r_halo, s_gx, r_gx, s_rel, r_rel, s_self,
    s_ax, r_ax, s_ay, r_ay, s_by, r_by, s_bx, r_bx, s_bx2, r_bx2,
    s_z, r_z, s_c, r_c, s_o, r_o, s_keep,
):
    x, y, k, z, ctx = place()
    chip = x * 8 + y
    kk = 1 - k

    def dev(dx=0, dy=0, dz=0, dk=0):
        return (
            (((x + dx + 4) % 4) * 8 + (y + dy + 8) % 8) * 2 + (k + dk) % 2,
            (z + dz + 8) % 8,
        )

    sibling = dev(dk=1)
    following = ((ctx + 1) % 64, z)
    previous = ((ctx + 63) % 64, z)
    pending = []

    def send(src, dst, ssem, rsem, to):
        c = pltpu.make_async_remote_copy(
            src_ref=src, dst_ref=dst, send_sem=ssem, recv_sem=rsem,
            device_id=to, device_id_type=MESH,
        )
        c.start()
        pending.append(c)

    def arrived_at(dst, ssem, rsem):
        pltpu.make_async_remote_copy(
            src_ref=dst, dst_ref=dst, send_sem=ssem, recv_sem=rsem,
            device_id=sibling, device_id_type=MESH,
        ).wait_recv()

    own_a = wa.at[y, x]
    own_b = wb.at[x, y]
    mine = pl.ds(pl.multiple_of(k * 64, 64), 64)

    def wcols(core, first, count):
        return w_in.at[:, pl.ds(pl.multiple_of(core * 512 + first, 128), count)]

    def start_weights():
        copies = (
            pltpu.make_async_copy(wcols(k, 0, ACOLS), own_a.at[mine], s_loc.at[0]),
            pltpu.make_async_copy(wcols(k, ACOLS, BCOLS), own_b.at[mine], s_loc.at[1]),
        )
        for c in copies:
            c.start()
        return copies

    load = pltpu.make_async_copy(feat_in, feat.at[:, pl.ds(16, ROWS)], s_feat)
    load.start()
    w_loads = start_weights()
    loads = [
        pltpu.make_async_copy(src, dst, s_in.at[n])
        for n, (src, dst) in enumerate(
            ((seg_in, seg_v), (tgt_in, tgt_v), (cost_in, cost_v),
             (taps_in, taps), (filt_in, filt), (gain_in, gain))
        )
    ]
    for c in loads:
        c.start()
    barrier = pltpu.get_barrier_semaphore()

    def greet(i, carry):
        other = (chip + i) % 32
        pl.semaphore_signal(barrier, inc=1, device_id=(other * 2 + k, z), device_id_type=MESH)
        return carry

    lax.fori_loop(1, 32, greet, 0)
    for to in (sibling, following, previous, dev(dz=1), dev(dz=-1)):
        pl.semaphore_signal(barrier, inc=1, device_id=to, device_id_type=MESH)

    for c in loads:
        c.wait()

    def row_of(ref, fill):
        return jnp.concatenate([ref[...].astype(F32), jnp.full((1, 96), fill, F32)], axis=1)

    seg_pad = row_of(seg_v, -7.0)
    meta[0:1, :] = seg_pad
    meta[1:2, :] = row_of(tgt_v, -7.0)
    meta[2:3, :] = row_of(cost_v, 0.0)
    meta[3:4, :] = pltpu.roll(seg_pad, 256 - 32, 1)
    meta[4:8, :] = jnp.zeros((4, 256), F32)
    metac = meta[...].T[0:ROWS]
    seg_col = metac[:, 0:1]
    tgt_col = metac[:, 1:2]
    cost_col = metac[:, 2:3]
    lag = iota((ROWS, 384), 0) + TAPS - iota((ROWS, 384), 1)
    in_reach = (lag >= 0) & (lag < TAPS)

    def same_segment(prev_row):
        seg_row = jnp.concatenate([prev_row, meta[0:1, :]], axis=1)
        return jnp.where(in_reach & (seg_col == seg_row), 1.0, 0.0)

    def featurize(index, center, match_one, match_two):
        return (
            taps[index, 0:1, :] * center
            + taps[index, 1:2, :] * pltpu.roll(center, 1, 0) * match_one
            + taps[index, 2:3, :] * pltpu.roll(center, 2, 0) * match_two
        )

    seg_own = same_segment(jnp.full((1, 128), -1.0, F32))
    back = jnp.sum(seg_own, axis=1, keepdims=True)
    m_one = jnp.where(back > 1.5, 1.0, 0.0)
    m_two = jnp.where(back > 2.5, 1.0, 0.0)
    load.wait()
    own_rows = pl.ds(16, ROWS)
    qf[...] = featurize(0, feat[0, own_rows].astype(F32), m_one, m_two)
    win[pl.ds(128, ROWS), :] = (
        featurize(1, feat[1, own_rows].astype(F32), m_one, m_two)
        * featurize(2, feat[2, own_rows].astype(F32), m_one, m_two)
    ).astype(BF)
    win[pl.ds(288, 96), :] = jnp.zeros((96, 512), BF)

    mine_rows = pl.ds(pl.multiple_of(k * ROWS, 16), ROWS)
    pl.semaphore_wait(barrier, 36)

    send(wcols(kk, 0, ACOLS), own_a.at[mine], s_sib.at[0], r_sib.at[0], sibling)
    send(wcols(kk, ACOLS, BCOLS), own_b.at[mine], s_sib.at[1], r_sib.at[1], sibling)
    send(feat.at[:, pl.ds(160, 16)], feat.at[:, pl.ds(0, 16)], s_halo.at[0], r_halo.at[0], following)
    send(meta, prevmeta, s_halo.at[1], r_halo.at[1], following)
    send(win.at[pl.ds(160, 128)], win.at[pl.ds(0, 128)], s_halo.at[2], r_halo.at[2], following)
    events = []

    def at(when, what, *args):
        events.append((when, len(events), functools.partial(what, *args)))

    def ranks():
        tgt_row = meta[1:2, :]
        same_target = tgt_col == tgt_row
        rq = iota((ROWS, 256), 0)
        rr = iota((ROWS, 256), 1)
        rank_row = jnp.sum(jnp.where(same_target & (rq < rr), 1.0, 0.0), axis=0, keepdims=True)
        rank_col = jnp.sum(jnp.where(same_target & (rr < rq), 1.0, 0.0), axis=1, keepdims=True)
        kf = k.astype(F32)
        chip_row = jnp.floor(tgt_row * 0.5)
        chip_col = jnp.floor(tgt_col * 0.5)
        i_row = (tgt_row - 2.0 * chip_row) * 10.0 + kf * 5.0 + rank_row
        i_col = (tgt_col - 2.0 * chip_col) * 10.0 + kf * 5.0 + rank_col
        first = chip_row * 16.0
        slots[k, 0:1, :] = jnp.where(i_row < 15.5, first + i_row, -1.0)
        slots[k, 1:2, :] = jnp.where(i_row > 15.5, first + i_row - 16.0, -1.0)
        slots[k, 2:3, :] = jnp.where(i_row > 15.5, first + i_row - 12.0, -1.0)
        slots[k, 3:4, :] = first + 8.0
        slots[k, 4:8, :] = jnp.zeros((4, 256), F32)
        cbuf[mine_rows, :] = jnp.where(
            iota((ROWS, 128), 1).astype(F32) == i_col, cost_col, 0.0
        ).astype(BF)
        send(slots.at[k], slots.at[k], s_gx.at[1], r_gx.at[1], sibling)
        send(cbuf.at[mine_rows], cbuf.at[mine_rows], s_gx.at[2], r_gx.at[2], sibling)

    def filters():
        flip = (iota((TAPS, TAPS), 0) + iota((TAPS, TAPS), 1)) % TAPS == 0
        hrev[...] = jnp.dot(
            filt[...].astype(BF), jnp.where(flip, 1.0, 0.0).astype(BF), preferred_element_type=F32
        )

        def turn(i, carry):
            for n in range(4):
                row = jnp.broadcast_to(hrev[pl.ds(i * 4 + n, 1), :], (TAPS, TAPS))
                circ[i * 4 + n] = pltpu.roll(row, 0, 1, stride=1, stride_axis=0).astype(BF)
            return carry

        lax.fori_loop(0, 8, turn, 0)

    def w_own():
        theirs = pl.ds(pl.multiple_of(kk * 64, 64), 64)
        for c in w_loads:
            c.wait()
        arrived_at(own_a.at[theirs], s_sib.at[0], r_sib.at[0])
        arrived_at(own_b.at[theirs], s_sib.at[1], r_sib.at[1])
        for d in (1, 2, 3):
            send(own_a, own_a, s_ax.at[d - 1], r_ax.at[d - 1], dev(dx=d))
        by_send(1)
        bx_send(0)

    def by_piece(t, way):
        ref = wb.at[x, (y + (1 - t if way == 0 else t - 1) + 8) % 8]
        return ref if t < 4 else ref.at[pl.ds(way * 64, 64)]

    def by_landed(t, way):
        ref = wb.at[x, (y + (-t if way == 0 else t) + 8) % 8]
        return ref if t < 4 else ref.at[pl.ds(way * 64, 64)]

    def by_send(t):
        for way in (0, 1):
            piece = by_piece(t, way)
            send(piece, piece, s_by.at[way, t - 1], r_by.at[way, t - 1], dev(dy=1 - 2 * way))

    def by_step(t):
        for way in (0, 1):
            arrived_at(by_landed(t, way), s_by.at[way, t - 1], r_by.at[way, t - 1])
        if t < 4:
            bx_send(2 * t - 1)
            bx_send(2 * t)
        else:
            bx_send(7)

    def ay_part(off, h):
        return wa.at[(y + off + 8) % 8, pl.ds(2 * h, 2)]

    def ay_ways(t, h):
        return (0, 1) if t < 4 else (h,)

    def ay_send(t, h):
        for way in ay_ways(t, h):
            piece = ay_part(1 - t if way == 0 else t - 1, h)
            send(
                piece, piece, s_ay.at[way, t - 1, h], r_ay.at[way, t - 1, h], dev(dy=1 - 2 * way)
            )

    def ax_done():
        for d in (1, 2, 3):
            arrived_at(wa.at[y, (x - d + 4) % 4], s_ax.at[d - 1], r_ax.at[d - 1])
        for h in (0, 1):
            ay_send(1, h)

    def ay_step(t):
        for h in (0, 1):
            for way in ay_ways(t, h):
                landed = ay_part(-t if way == 0 else t, h)
                arrived_at(landed, s_ay.at[way, t - 1, h], r_ay.at[way, t - 1, h])
            if t < 4:
                ay_send(t + 1, h)

    def bx_row(j):
        return (y + offset_of(j) + 8) % 8

    def bx_send(j):
        piece = wb.at[x, bx_row(j)]
        for way in (0, 1):
            send(piece, piece, s_bx.at[way, j], r_bx.at[way, j], dev(dx=1 - 2 * way))

    def bx_step(j):
        for way in (0, 1):
            landed = wb.at[(x + 2 * way - 1 + 4) % 4, bx_row(j)]
            arrived_at(landed, s_bx.at[way, j], r_bx.at[way, j])
        way = j % 2
        piece = wb.at[(x + 2 * way - 1 + 4) % 4, bx_row(j)]
        send(piece, piece, s_bx2.at[j], r_bx2.at[j], dev(dx=1 - 2 * way))

    def w_last():
        for j in range(8):
            arrived_at(wb.at[(x + 2) % 4, bx_row(j)], s_bx2.at[j], r_bx2.at[j])

    def halo():
        arrived_at(prevmeta, s_halo.at[1], r_halo.at[1])
        arrived_at(feat.at[:, pl.ds(0, 16)], s_halo.at[0], r_halo.at[0])
        prev_row = jnp.where(ctx == 0, -1.0, prevmeta[3:4, 0:128])
        mask = same_segment(prev_row)
        mask_a[...] = mask[0:128, 0:256].astype(BF)
        mask_b[...] = mask[128:160, 128:384].astype(BF)
        count = jnp.sum(mask[0:32], axis=1, keepdims=True)[0:16]
        one = jnp.where(count > 1.5, 1.0, 0.0)
        two = jnp.where(count > 2.5, 1.0, 0.0)
        pad = jnp.zeros((16, 1), F32)
        one = jnp.concatenate([pad, one], axis=0)
        two = jnp.concatenate([pad, two], axis=0)
        fixed = [
            featurize(i, feat[i, pl.ds(0, 32)].astype(F32), one, two)[16:32] for i in range(3)
        ]
        qf[pl.ds(0, 16), :] = fixed[0]
        win[pl.ds(128, 16), :] = (fixed[1] * fixed[2]).astype(BF)
        arrived_at(win.at[pl.ds(0, 128)], s_halo.at[2], r_halo.at[2])

    def conv(part, dst, dst_rows):
        lane_group = iota((TAPS, 128), 1) // 16
        for tile in range(2):
            cols = pl.ds(pl.multiple_of(part * 256 + tile * 128, 128), 128)
            tall, low = [], []
            for n in range(8):
                turned = circ[part * 16 + tile * 8 + n]
                pair = jnp.concatenate([turned, turned], axis=1)
                tall.append(pair * mask_a[...])
                low.append(pair[0:32] * mask_b[...])
            res_a = jnp.dot(
                jnp.concatenate(tall, axis=0), win[pl.ds(0, 256), cols], preferred_element_type=F32
            )
            res_b = jnp.dot(
                jnp.concatenate(low, axis=0), win[pl.ds(128, 256), cols], preferred_element_type=F32
            )
            top, bottom = res_a[0:128], res_b[0:32]
            for n in range(1, 8):
                top = jnp.where(lane_group == n, res_a[n * 128:(n + 1) * 128], top)
                bottom = jnp.where(lane_group[0:32] == n, res_b[n * 32:(n + 1) * 32], bottom)
            total = jnp.concatenate([top, bottom], axis=0)
            center = win[pl.ds(128, ROWS), cols].astype(F32)
            dst[dst_rows, pl.ds(tile * 128, 128)] = (
                qf[:, cols] * (total + gain[:, cols] * center)
            ).astype(BF)

    def conv_theirs():
        conv(kk, gsend, pl.ds(0, ROWS))
        send(gsend, gbuf.at[mine_rows], s_gx.at[0], r_gx.at[0], sibling)

    def conv_mine():
        conv(k, gbuf, mine_rows)

    def unit_rows(u):
        return pl.ds(u * UNIT_ROWS, UNIT_ROWS)

    own_block = pl.ds(pl.multiple_of(chip * 16, 16), 16)

    def keep_own():
        return pltpu.make_async_copy(packed.at[own_block], arrived.at[own_block], s_self)

    def pack():
        other_rows = pl.ds(pl.multiple_of(kk * ROWS, 16), ROWS)
        arrived_at(slots.at[kk], s_gx.at[1], r_gx.at[1])
        arrived_at(cbuf.at[other_rows], s_gx.at[2], r_gx.at[2])
        place_row = iota((512, 2 * ROWS), 0).astype(F32)

        def pick(n):
            slot = jnp.concatenate([slots[0, n:n + 1, 0:ROWS], slots[1, n:n + 1, 0:ROWS]], axis=1)
            return jnp.where(place_row == slot, 1.0, 0.0).astype(BF)

        arrived_at(gbuf.at[other_rows], s_gx.at[0], r_gx.at[0])
        packed[:, 0:256] = jnp.dot(pick(0), gbuf[...], preferred_element_type=F32).astype(BF)
        packed[:, 256:384] = (
            jnp.dot(pick(1), gbuf[:, 0:128], preferred_element_type=F32)
            + jnp.dot(pick(2), gbuf[:, 128:256], preferred_element_type=F32)
            + jnp.dot(pick(3), cbuf[...], preferred_element_type=F32)
        ).astype(BF)
        keep_own().start()

        def post(i, carry):
            other = ((x + i // 8 + i % 8) % 4) * 8 + (y + offset_of(7 - i % 8) + 8) % 8
            pltpu.make_async_remote_copy(
                src_ref=packed.at[pl.ds(pl.multiple_of(other * 16, 16), 16)],
                dst_ref=arrived.at[own_block], send_sem=s_rel, recv_sem=r_rel,
                device_id=(other * 2 + k, z), device_id_type=MESH,
            ).start()
            return carry

        lax.fori_loop(0, 15, post, 0)
        lax.fori_loop(16, 32, post, 0)

    def relay_wait():
        bulk = pltpu.make_async_remote_copy(
            src_ref=packed.at[pl.ds(0, 496)], dst_ref=arrived.at[pl.ds(0, 496)],
            send_sem=s_rel, recv_sem=r_rel, device_id=sibling, device_id_type=MESH,
        )
        bulk.wait_send()
        bulk.wait_recv()
        keep_own().wait()

    def unpack():
        col = iota((1, 512), 1) % 16
        spread_i = iota((128, 512), 0)
        spread_c = iota((128, 512), 1) % 16
        spread_a = jnp.where(spread_i == spread_c, 1.0, 0.0).astype(BF)
        spread_b = jnp.where((spread_c < 8) & (spread_i == 16 + spread_c % 4), 1.0, 0.0).astype(BF)
        mine_only = iota((32, 512), 0) == iota((32, 512), 1) // 16
        pickc = jnp.where(iota((32, 512), 1) == iota((32, 512), 0) * 16 + 8, 1.0, 0.0).astype(BF)
        a = iota((128, 128), 0)
        b = iota((128, 128), 1)
        both = (a // 10 == b // 10) & (a % 5 == 0) & (b < 20)
        first = both & (a % 10 == 0) & (b % 10 >= 5)
        both = jnp.where(both, 1.0, 0.0).astype(BF)
        first = jnp.where(first, 1.0, 0.0).astype(BF)
        lower = jnp.where(iota((32, 32), 1) < iota((32, 32), 0), 1.0, 0.0).astype(BF)
        lane = iota((32, 128), 1)
        relay_wait()
        costs = jnp.dot(pickc, arrived[:, 256:384], preferred_element_type=F32)
        mine_lane = (lane >= k * 10) & (lane < k * 10 + 10)
        cost_out[0] = jnp.sum(jnp.where(mine_lane, costs, 0.0)) / (32.0 * ROWS)
        live = jnp.where(costs > 0.5, 1.0, 0.0).astype(BF)
        tally = jnp.dot(live, both, preferred_element_type=F32)
        before = jnp.dot(live, first, preferred_element_type=F32)
        rank = jnp.dot(lower, tally.astype(BF), preferred_element_type=F32) + before
        code = jnp.where(costs > 0.5, rank + 1.0, 0.0).astype(BF)

        def dest_row(spread, i):
            wide = jnp.dot(code, spread, preferred_element_type=F32)
            code_row = jnp.sum(jnp.where(mine_only, wide, 0.0), axis=0, keepdims=True)
            dest = ((i // 10) * ROWS + i % 5).astype(F32) + 5.0 * (code_row - 1.0)
            return jnp.where(code_row > 0.5, dest, -1.0)

        dest_a = dest_row(spread_a, col)
        dest_b = dest_row(spread_b, 16 + col % 4)
        dest_lo = jnp.where(col < 4, dest_b, -1.0)
        dest_hi = jnp.where(col >= 4, dest_b, -1.0)
        target = iota((ROWS, 512), 0).astype(F32)
        for part in range(2):

            def hit(dest):
                return jnp.where(target == dest - float(part * ROWS), 1.0, 0.0).astype(BF)

            main = jnp.dot(hit(dest_a), arrived[:, 0:256], preferred_element_type=F32)
            low = jnp.dot(hit(dest_lo), arrived[:, 256:384], preferred_element_type=F32)
            high = jnp.dot(hit(dest_hi), arrived[:, 256:384], preferred_element_type=F32)
            rows = jnp.concatenate([main[:, 0:128] + low, main[:, 128:256] + high], axis=1)
            abuf[z * 2 + k, pl.ds(part * ROWS, ROWS), :] = rows.astype(BF)
            for u in (2 * part, 2 * part + 1):
                z_send(u, 1)
        for u in range(UNITS):
            mine_slot = abuf.at[z * 2 + k, unit_rows(u)]
            send(mine_slot, mine_slot, s_c.at[u, 0], r_c.at[u, 0], sibling)

    def z_slot(u, off, core):
        return abuf.at[((z + off + 8) % 8) * 2 + core, unit_rows(u)]

    def z_ways(u, t):
        return (0, 1) if t < 4 else (u // 2,)

    def z_send(u, t):
        for way in z_ways(u, t):
            piece = z_slot(u, 1 - t if way == 0 else t - 1, k)
            send(piece, piece, s_z.at[u, way, t - 1], r_z.at[u, way, t - 1], dev(dz=1 - 2 * way))

    def z_step(t, *units):
        for u in units:
            for way in z_ways(u, t):
                landed = z_slot(u, -t if way == 0 else t, k)
                arrived_at(landed, s_z.at[u, way, t - 1], r_z.at[u, way, t - 1])
            if t < 4:
                z_send(u, t + 1)
            for j in ((2 * t - 1, 2 * t) if t < 4 else (7,)):
                piece = z_slot(u, offset_of(j), k)
                send(piece, piece, s_c.at[u, j], r_c.at[u, j], sibling)

    def multiply(part, wait):
        part_rows = pl.ds(pl.multiple_of(part * ROWS, 16), ROWS)

        def step(i, carry):
            rows, weights = [], []
            for n in range(2):
                j = 2 * i + n
                zo = (z + offset_of(j) + 8) % 8
                for u in range(UNITS if wait else 0):
                    arrived_at(abuf.at[zo * 2 + kk, unit_rows(u)], s_c.at[u, j], r_c.at[u, j])
                xs = zo // 2
                for half in (0, 1):
                    rows.append(abuf[zo * 2 + half, part_rows, :])
                    for m in (0, 1):
                        ys = (zo % 2) * 4 + 2 * half + m
                        weights.append(jnp.concatenate([wa[ys, xs], wb[xs, ys]], axis=1))
            acc[part_rows, :] += jnp.dot(
                jnp.concatenate(rows, axis=1), jnp.concatenate(weights, axis=0),
                preferred_element_type=F32,
            )
            return carry

        lax.fori_loop(0, 4, step, 0)

    def clear():
        acc[...] = jnp.zeros_like(acc)

    def finish():
        cols = pl.ds(pl.multiple_of(k * 512, 512), 512)
        theirs = pl.ds(pl.multiple_of(kk * ROWS, 16), ROWS)
        multiply(kk, True)
        osend[...] = acc[theirs, :].astype(BF)
        send(osend, out.at[:, cols], s_o, r_o, sibling)
        multiply(k, False)
        okeep[...] = acc[mine_rows, :].astype(BF)
        keep = pltpu.make_async_copy(okeep, out.at[:, cols], s_keep)
        keep.start()
        keep.wait()
        arrived_at(out.at[:, pl.ds(pl.multiple_of(kk * 512, 512), 512)], s_o, r_o)

    plan = (
        (w_own, 1),
        (ranks, 2),
        (filters, 3),
        (halo, 4),
        (conv_theirs, 5),
        (conv_mine, 6),
        (by_step, 7, 1),
        (by_send, 8, 2),
        (pack, 9),
        (ax_done, 10),
        (bx_step, 11, 0),
        (by_step, 12, 2),
        (by_send, 13, 3),
        (bx_step, 14, 1),
        (bx_step, 15, 2),
        (clear, 16),
        (unpack, 17),
        (bx_step, 18, 3),
        (bx_step, 19, 4),
        (ay_step, 20, 1),
        (by_step, 21, 3),
        (by_send, 22, 4),
        (z_step, 23, 1, 0, 1),
        (z_step, 24, 1, 2, 3),
        (by_step, 25, 4),
        (ay_step, 26, 2),
        (z_step, 27, 2, 0, 1),
        (bx_step, 28, 5),
        (bx_step, 29, 6),
        (z_step, 30, 2, 2, 3),
        (bx_step, 31, 7),
        (ay_step, 32, 3),
        (z_step, 33, 3, 0, 1),
        (z_step, 34, 3, 2, 3),
        (z_step, 35, 4, 0, 1),
        (z_step, 36, 4, 2, 3),
        (ay_step, 37, 4),
        (w_last, 38),
        (finish, 39),
    )
    for what, when, *args in plan:
        at(when, what, *args)
    for _, _, run in sorted(events, key=lambda e: e[:2]):
        run()
    for c in pending:
        c.wait_send()


def local(features, segment_ids, feat_taps, mixer_filter, skip_gain, out_weight, targets, row_costs):
    parts = jnp.transpose(features, (1, 0, 2))
    vmem = pl.BlockSpec(memory_space=pltpu.VMEM)
    hbm = pl.BlockSpec(memory_space=pltpu.HBM)
    dma = pltpu.SemaphoreType.DMA
    u = UNITS
    flops = 2 * 320 * 4096 * 512
    out, cost_out = pl.pallas_call(
        mixer_kernel,
        out_shape=(
            jax.ShapeDtypeStruct((ROWS, 1024), BF),
            jax.ShapeDtypeStruct((1,), F32),
        ),
        in_specs=[hbm] * 8,
        out_specs=(hbm, pl.BlockSpec(memory_space=pltpu.SMEM)),
        scratch_shapes=[
            pltpu.VMEM((3, 3, 512), F32),
            pltpu.VMEM((32, TAPS), F32),
            pltpu.VMEM((1, 512), F32),
            pltpu.VMEM((1, ROWS), jnp.int32),
            pltpu.VMEM((1, ROWS), jnp.int32),
            pltpu.VMEM((1, ROWS), jnp.int32),
            pltpu.VMEM((8, 256), F32),
            dma((6,)),
            pltpu.VMEM((3, 16 + ROWS, 512), BF),
            pltpu.VMEM((ROWS, 512), F32),
            pltpu.VMEM((384, 512), BF),
            pltpu.VMEM((32, 128), F32),
            pltpu.VMEM((32, TAPS, TAPS), BF),
            pltpu.VMEM((128, 256), BF),
            pltpu.VMEM((32, 256), BF),
            pltpu.VMEM((ROWS, 256), BF),
            pltpu.VMEM((2 * ROWS, 256), BF),
            pltpu.VMEM((2 * ROWS, 128), BF),
            pltpu.VMEM((2, 8, 256), F32),
            pltpu.VMEM((8, 256), F32),
            pltpu.VMEM((512, 384), BF),
            pltpu.VMEM((512, 384), BF),
            pltpu.VMEM((16, 2 * ROWS, 256), BF),
            pltpu.VMEM((8, 4, 128, ACOLS), BF),
            pltpu.VMEM((4, 8, 128, BCOLS), BF),
            pltpu.VMEM((2 * ROWS, 512), F32),
            pltpu.VMEM((ROWS, 512), BF),
            pltpu.VMEM((ROWS, 512), BF),
            dma, dma((2,)), dma((2,)), dma((2,)), dma((3,)), dma((3,)), dma((3,)), dma((3,)),
            dma, dma, dma,
            dma((3,)), dma((3,)), dma((2, 4, 2)), dma((2, 4, 2)), dma((2, 4)), dma((2, 4)),
            dma((2, 8)), dma((2, 8)), dma((8,)), dma((8,)),
            dma((u, 2, 4)), dma((u, 2, 4)), dma((u, 8)), dma((u, 8)), dma, dma, dma,
        ],
        compiler_params=pltpu.CompilerParams(
            collective_id=0, has_side_effects=True, vmem_limit_bytes=60 * 2**20
        ),
        cost_estimate=pl.CostEstimate(flops=flops, bytes_accessed=16 * 2**20, transcendentals=0),
        name="mixer",
    )(
        parts, out_weight, feat_taps, mixer_filter, skip_gain[None, :],
        segment_ids[None, :], targets[None, :], row_costs[None, :],
    )
    return out, cost_out


def solution(mesh):
    placed = (
        P("ctx", None, "ch"),
        P("ctx"),
        P(None, None, "ch"),
        P("ch", None),
        P("ch"),
        P("ctx", "ch"),
        P("ctx"),
        P("ctx"),
    )
    return jax.shard_map(
        local, mesh=mesh, in_specs=placed, out_specs=(P("ctx", "ch"), P("ctx")), check_vma=False
    )
```
